256 devices in a mesh: pipe: 16 (over x, z_hi), tensor: 16 (over z_lo, y, core).
Axes of the slice: x: 4, y: 4, z: 8 (z_hi: 4, z_lo: 2; z = z_hi * 2 + z_lo), core: 2. Of those that a mesh axis runs over, the one named last changes fastest.
Arguments:
- hidden_states: bfloat16 [512, 4608], P('tensor'), may hold values from -24 to 24
- embedding: bfloat16 [163840, 4608], P(('pipe', 'tensor')), may hold values from -3 to 3
- token_ids: int32 [512], P('tensor'), may hold values from 0 to 163839
- target_ids: int32 [512], P('tensor'), may hold values from 0 to 163839
- coefficients: bfloat16 [512], P('tensor'), may hold values from -48 to 48
- cotangent: bfloat16 [512, 4608], P('tensor'), may hold values from -0.3125 to 0.3125
- value_weight: bfloat16 [4608], replicated, may hold values from -0.625 to 0.625
- returns: float32 [512], P('tensor'), may hold values from -32 to 32
Outputs:
- grad_embedding: bfloat16 [163840, 4608], P(('pipe', 'tensor'))
- grad_hidden: bfloat16 [512, 4608], P('tensor')
- grad_value: float32 [4608], replicated
The draws below stay inside these ranges and needn't reach their ends.
All inputs are finite; a program needn't handle non-finite values.
Results may differ from the reference program's by a relative error of at most 0.0034.
Values may be sent and summed in bfloat16 or wider, within the bound.
A program may use at most 128 MiB of HBM per device.

```python
import math
import jax
import jax.numpy as jnp
import numpy as np
from jax import lax

D = 4608
VOC_DEV = 640
TOKENS = 512
VOCAB = 163840
N_PIPE = 16
N_TENSOR = 16


def draw_embedding(key, part):
    key = jax.random.fold_in(key, 1)
    row_index = jnp.arange(VOCAB)
    matrix = jnp.clip(jax.random.normal(key, (VOCAB, D)), -6.0, 6.0) * (3.0 * D ** (-0.5)) * (1.0 + 0.2 * row_index / VOCAB)[:, None]
    return matrix.astype(jnp.bfloat16)


def draw_hidden_states(key, part):
    key = jax.random.fold_in(key, 2)
    matrix = jnp.clip(jax.random.normal(key, (TOKENS, D)), -6.0, 6.0)
    return matrix.astype(jnp.bfloat16)


def place_ends(drawn, rng, low, high):
    shape = drawn.shape
    index_at = [jax.random.randint(jax.random.fold_in(rng, axis), (), 0, shape[axis]) for axis in range(len(shape))]
    drawn = drawn.at[tuple(index_at)].set(low)
    longest = shape.index(max(shape))
    index_at[longest] = (index_at[longest] + 1) % shape[longest]
    return drawn.at[tuple(index_at)].set(high)


def block_levels(key, dims, pieces, smallest, top_value):
    loudness = 1.0
    for position, parts in pieces:
        heights = jax.random.uniform(jax.random.fold_in(jax.random.fold_in(key, 6), position), (parts,), jnp.float32, smallest / len(pieces), top_value / len(pieces))
        loudness = loudness * jnp.repeat(jnp.exp(heights), dims[position] // parts).reshape((-1,) + (1,) * (len(dims) - 1 - position))
    return loudness


def ranked_wide(rng, extent, number_of, skew):
    loads = [min(1 << octave, number_of + 1 - (1 << octave)) * (1 << 20) // math.isqrt((1 << octave) ** skew) + 1 for octave in range((number_of + 1).bit_length()) if 1 << octave <= number_of]
    width = 1 + sum(loads) // (1 << 30)
    listing = np.cumsum(np.array([max(1, weight // width) for weight in loads]))
    ticket = jax.random.randint(jax.random.fold_in(rng, 1), extent, 0, int(listing[len(loads) - 1]))
    start = jnp.left_shift(1, jnp.searchsorted(jnp.asarray(listing, jnp.int32), ticket, side="right").astype(jnp.int32))
    grade = start - 1 + jax.random.randint(jax.random.fold_in(rng, 4), extent, 0, 1 << 30) % jnp.minimum(start, number_of + 1 - start)
    return jax.random.permutation(jax.random.fold_in(rng, 2), number_of)[grade].astype(jnp.int32)


def normal_values(stream_key, dims, width, most, cuts=(), held_as=jnp.bfloat16):
    values = width * jax.random.normal(stream_key, dims, jnp.float32)
    if cuts:
        values = values * block_levels(stream_key, dims, cuts, -0.22, 0.18)
    return jnp.clip(values, -most, most).astype(held_as)


def setup_inputs(seed: int = 0) -> dict:
    seeds = jax.random.split(jax.random.key(seed), 9)
    hidden_states = draw_hidden_states(jax.random.fold_in(seeds[8], 71), 0)
    embedding = draw_embedding(jax.random.fold_in(seeds[8], 71), 0)
    token_ids = place_ends(ranked_wide(seeds[2], (TOKENS,), VOCAB, 2), jax.random.fold_in(seeds[2], 3), 0, VOCAB - 1).astype(jnp.int32)
    target_ids = place_ends(ranked_wide(seeds[3], (TOKENS,), VOCAB, 2), jax.random.fold_in(seeds[3], 3), 0, VOCAB - 1).astype(jnp.int32)
    coefficients = normal_values(seeds[4], (TOKENS,), 8.0, 48.0, ((0, 16),))
    cotangent = normal_values(seeds[5], (TOKENS, D), 0.05, 0.3125, ((0, 16),))
    value_weight = normal_values(seeds[6], (D,), 0.1, 0.625)
    returns = normal_values(seeds[7], (TOKENS,), 6.0, 32.0, ((0, 16),), jnp.float32)
    return {"hidden_states": hidden_states, "embedding": embedding, "token_ids": token_ids, "target_ids": target_ids, "coefficients": coefficients, "cotangent": cotangent, "value_weight": value_weight, "returns": returns}


VALUE_SCALE = 0.5

def reference(hidden_states, embedding, token_ids, target_ids, coefficients, cotangent, value_weight, returns):
    logits = lax.dot_general(hidden_states, embedding, (((1,), (1,)), ((), ())), preferred_element_type=jnp.float32)
    row_peak = lax.optimization_barrier(jnp.max(logits, axis=1, keepdims=True))
    weights = jnp.exp(logits - row_peak)
    row_total = lax.optimization_barrier(jnp.sum(weights, axis=1, keepdims=True))
    vocab_index = lax.broadcasted_iota(jnp.int32, (1, embedding.shape[0]), 1)
    target_hit = (target_ids[:, None] == vocab_index).astype(jnp.float32)
    logit_grad = (coefficients.astype(jnp.float32)[:, None] * (weights / row_total - target_hit)).astype(jnp.bfloat16)
    value_out = jnp.dot(hidden_states, value_weight, preferred_element_type=jnp.float32)
    value_delta = VALUE_SCALE * (value_out - returns)
    summed = jnp.dot(logit_grad, embedding, preferred_element_type=jnp.float32)
    grad_hidden = (summed + value_delta[:, None] * value_weight.astype(jnp.float32)[None, :]).astype(jnp.bfloat16)
    grad_value = jnp.dot(value_delta, hidden_states.astype(jnp.float32), precision=lax.Precision.HIGHEST)
    normalizer = math.sqrt(D)
    cotangent_wide = cotangent.astype(jnp.float32)

    def one_block(block):
        first_row = (block * VOC_DEV).astype(jnp.int32)
        grads = lax.dynamic_slice_in_dim(logit_grad, first_row, VOC_DEV, 1)
        head_term = lax.dot_general(grads, hidden_states, (((0,), (0,)), ((), ())), preferred_element_type=jnp.float32)
        lookup_table = (token_ids[:, None] == first_row + lax.broadcasted_iota(jnp.int32, (1, VOC_DEV), 1)).astype(jnp.float32)
        looked = lax.dot_general(lookup_table, cotangent_wide, (((0,), (0,)), ((), ())), precision=lax.Precision.HIGHEST)
        return (head_term + normalizer * looked).astype(jnp.bfloat16)
    blocks = lax.map(one_block, jnp.arange(N_PIPE * N_TENSOR, dtype=jnp.int32))
    grad_embedding = blocks.reshape(VOCAB, D)
    return (grad_embedding, grad_hidden, grad_value)
```

```python
import math

import jax
import jax.numpy as jnp
from jax import lax
from jax.experimental import pallas as pl
from jax.experimental.pallas import tpu as pltpu
from jax.sharding import PartitionSpec as P

VALUE_SCALE = 0.5
MESH = pl.DeviceIdType.MESH
F32, BF16 = jnp.float32, jnp.bfloat16

ROWS = 32
TOK = 512
D = 4608
HALF = D // 2
PIECE = 768
QUART = PIECE // 2
VOC = 640
W = HALF // 2
SENDS = 224


def align(value, to=128):
    return pl.multiple_of(value, to)


def kernel(
    hs, emb, tid, tgt, coef, cot, vw, ret,
    ge, gh, gv,
    H, C, E, EH, LT, GS, GT, PA, PB, SA, SB, RA, RB, SA2, SB2, RA2, RB2,
    ZS, ZR, FZ, OUT, META, STA, RSA, STB, RSB, VB, VR, GO,
    ss, rs, ls, xs,
):
    pipe, tensor = lax.axis_index("pipe"), lax.axis_index("tensor")
    x, zh = pipe // 4, pipe % 4
    zl, y, c = tensor // 8, (tensor // 2) % 4, tensor % 2
    z = 2 * zh + zl
    q = x % 2

    def dev(dx=0, dy=0, dz=0, dc=0):
        xx, yy, zz, cc = (x + dx) % 4, (y + dy) % 4, (z + dz + 8) % 8, (c + dc) % 2
        return xx * 4 + zz // 2, (zz % 2) * 8 + yy * 2 + cc

    pair = 1 - 2 * zl

    counter = [0]
    started = []

    def send(src, dst, target):
        k = counter[0]
        counter[0] += 1
        cp = pltpu.make_async_remote_copy(
            src_ref=src, dst_ref=dst, send_sem=ss.at[k], recv_sem=rs.at[k],
            device_id=target, device_id_type=MESH,
        )
        cp.start()
        started.append(cp)
        return cp

    def load(src, dst, k):
        cp = pltpu.make_async_copy(src, dst, ls.at[k])
        cp.start()
        return cp

    my_half = pl.ds(align(c * HALF), HALF)
    sib_half = pl.ds(align((1 - c) * HALF), HALF)
    ld_h = load(hs, H.at[0, 0, 0], 0)
    ld_e = load(emb, E, 1)
    ld_c = load(cot, C.at[0, 0, 0], 2)
    ld_eh = load(emb.at[:, my_half], EH.at[0:VOC], 3)

    plane = [(dx, dy) for dx in range(4) for dy in range(4) if (dx, dy) != (0, 0)]
    column = [(dz, dc) for dz in range(8) for dc in range(2) if (dz, dc) != (0, 0)]
    peers = [(dx, dy, 0, 0) for dx, dy in plane] + [(0, 0, dz, dc) for dz, dc in column]
    peers += [(dx, 0, 0, 1) for dx in (1, 2, 3)]
    bar = pltpu.get_barrier_semaphore()
    for peer in peers:
        pl.semaphore_signal(bar, inc=1, device_id=dev(*peer), device_id_type=MESH)

    META[0, 0, 0] = jnp.zeros((8, 128), F32)
    META[0, 0, 0, 0:1, 0:ROWS] = tid[...].astype(F32)
    META[0, 0, 0, 1:2, 0:ROWS] = tgt[...].astype(F32)
    META[0, 0, 0, 2:3, 0:ROWS] = coef[...].astype(F32)
    pl.semaphore_wait(bar, len(peers))

    def cols(half, j):
        return pl.ds(align(half * HALF + j * PIECE), PIECE)

    def quarter(half, j, k):
        return pl.ds(align(half * HALF + j * PIECE + k * QUART), QUART)

    class Gather:
        def __init__(self, X):
            self.X = X
            self.m = {}

        def begin(self):
            X, m = self.X, self.m
            for j in range(3):
                m["za", j] = send(X.at[0, 0, 0, :, cols(q, j)], X.at[0, 1, 0, :, cols(q, j)], dev(dz=1))
                self.ysend(0, j)
                m["zb", j] = send(X.at[0, 0, 0, :, cols(1 - q, j)], X.at[0, 1, 0, :, cols(1 - q, j)], dev(dz=-1))
                if j == 0:
                    m["s0"] = send(X.at[0, 0, 0], X.at[0, 0, 1], dev(dc=1))

        def ysend(self, dz, j):
            X, m = self.X, self.m
            for dy in (1, 3, 2):
                part = X.at[0, dz, 0, :, cols(q, j)]
                m["y", dz, dy, j] = send(part, X.at[dy, dz, 0, :, cols(q, j)], dev(dy=-dy))

        def s1(self, j):
            X, m = self.X, self.m
            m["za", j].wait_recv()
            self.ysend(1, j)
            m["zb", j].wait_recv()
            for h, k in ((q, "sza"), (1 - q, "szb")):
                m[k, j] = send(X.at[0, 1, 0, :, cols(h, j)], X.at[0, 1, 1, :, cols(h, j)], dev(dc=1))

        def relay(self, dz, j):
            X, m = self.X, self.m
            for dy in (1, 2, 3):
                m["y", dz, dy, j].wait_recv()
            rows = pl.ds(1, 3)
            for k, dx in ((0, 1), (1, -1)):
                part = X.at[rows, dz, 0, :, quarter(q, j, k)]
                m["x", dz, k, j] = counter[0]
                send(part, part, dev(dx=dx))
            m["sy", dz, j] = send(
                X.at[rows, dz, 0, :, cols(q, j)], X.at[rows, dz, 1, :, cols(q, j)], dev(dc=1)
            )

        def s4(self, j):
            X, m = self.X, self.m
            rows = pl.ds(1, 3)
            for dz in range(2):
                for k in range(2):
                    part = X.at[rows, dz, 0, :, quarter(1 - q, j, k)]
                    pltpu.make_async_remote_copy(
                        src_ref=part, dst_ref=part, send_sem=ss.at[m["x", dz, k, j]],
                        recv_sem=rs.at[m["x", dz, k, j]], device_id=dev(dc=1), device_id_type=MESH,
                    ).wait_recv()
                m["sx", dz, j] = send(
                    X.at[rows, dz, 0, :, cols(1 - q, j)], X.at[rows, dz, 1, :, cols(1 - q, j)], dev(dc=1)
                )

        def s5(self, j):
            m = self.m
            if j == 0:
                m["s0"].wait_recv()
            for k in ("sza", "szb"):
                m[k, j].wait_recv()
            for dz in range(2):
                m["sy", dz, j].wait_recv()
                m["sx", dz, j].wait_recv()

    gat_h, gat_c = Gather(H), Gather(C)

    ld_h.wait()
    gat_h.begin()

    h_own = H[0, 0, 0].astype(F32)
    value_out = jnp.sum(h_own * vw[...].astype(F32), axis=1, keepdims=True)
    eye = lax.broadcasted_iota(jnp.int32, (ROWS, ROWS), 0) == lax.broadcasted_iota(jnp.int32, (ROWS, ROWS), 1)
    ret_col = jnp.sum(jnp.where(eye, jnp.broadcast_to(ret[...], (ROWS, ROWS)), 0.0), axis=1, keepdims=True)
    delta = VALUE_SCALE * (value_out - ret_col)
    META[0, 0, 0, 3:4, 0:ROWS] = jnp.sum(jnp.where(eye, delta, 0.0), axis=0, keepdims=True)
    VB[0] = jnp.sum(delta * h_own, axis=0, keepdims=True)
    me_s = send(META.at[0, 0, 0], META.at[0, 0, 1], dev(dc=1))
    vv = [send(VB.at[0], VR.at[0], dev(dc=1))]

    gat_h.s1(0)
    gat_h.relay(0, 0)
    ld_e.wait()
    eh_s = send(E.at[:, sib_half], EH.at[VOC : 2 * VOC], dev(dc=1))
    gat_h.s1(1)
    gat_h.relay(1, 0)
    gat_h.relay(0, 1)
    me_s.wait_recv()
    me_z = send(META.at[0, 0], META.at[0, 1], dev(dz=pair))
    gat_h.s1(2)
    gat_h.relay(1, 1)
    gat_h.s4(0)
    gat_h.relay(0, 2)
    me_z.wait_recv()
    me_y = [send(META.at[0], META.at[dy], dev(dy=-dy)) for dy in (1, 2, 3)]
    vv[0].wait_recv()

    def value_step(k, target):
        VB[k] = VB[k - 1] + VR[k - 1]
        vv.append(send(VB.at[k], VR.at[k], target))

    value_step(1, dev(dz=pair))
    gat_h.s5(0)

    def logits(j):
        def tile(n, _):
            total = jnp.zeros((VOC, 256), F32)
            for half in range(2):
                at = half * HALF + j * PIECE
                rows = H[pl.ds(2 * n, 2), :, :, :, at : at + PIECE].reshape(256, PIECE)
                total += lax.dot_general(
                    E[:, at : at + PIECE], rows, (((1,), (1,)), ((), ())), preferred_element_type=F32
                )
            where = (slice(None), pl.ds(align(n * 256, 256), 256))
            LT[where] = total if j == 0 else LT[where] + total
            return 0

        lax.fori_loop(0, 2, tile, 0)

    logits(0)
    gat_h.relay(1, 2)
    gat_h.s4(1)
    ld_c.wait()
    gat_c.begin()
    gat_h.s5(1)
    logits(1)
    gat_h.s4(2)
    vv[1].wait_recv()
    value_step(2, dev(dy=1 - 2 * (y % 2)))
    gat_h.s5(2)
    logits(2)

    peak = jnp.max(LT[...], axis=0, keepdims=True)
    total = jnp.sum(jnp.exp(LT[...] - peak), axis=0, keepdims=True)
    STA[0:1] = peak
    STA[1:2] = total
    sta = {}
    for dx, dy in plane:
        back = (-dx % 4) * 4 + (-dy % 4)
        sta[back] = send(STA, RSA.at[back], dev(dx=dx, dy=dy))

    def merge(stats):
        peaks = stats[0][0]
        for p, _ in stats[1:]:
            peaks = jnp.maximum(peaks, p)
        sums = sum(s * jnp.exp(p - peaks) for p, s in stats)
        return peaks, sums

    gat_c.s1(0)
    gat_c.relay(0, 0)

    stats = [(peak, total)]
    for dx, dy in plane:
        k = dx * 4 + dy
        sta[k].wait_recv()
        got = RSA[k]
        if dy:
            got = jnp.concatenate([got[:, 128 * (4 - dy) :], got[:, : 128 * (4 - dy)]], axis=1)
        stats.append((got[0:1], got[1:2]))
    peak, total = merge(stats)
    STB[0:1] = peak
    STB[1:2] = total
    stb = {}
    for dz, dc in column:
        back = (-dz % 8) * 2 + dc
        stb[back] = send(STB, RSB.at[back], dev(dz=dz, dc=dc))

    gat_c.s1(1)
    gat_c.relay(1, 0)

    lane = lax.broadcasted_iota(jnp.int32, (2, 128), 1)

    def reorder(p, s, odd, dc):
        both = jnp.concatenate([p, s], axis=0)
        groups = []
        for g in range(4):
            part = both[:, 128 * g : 128 * (g + 1)]
            if odd:
                part = pltpu.roll(part, 64, 1)
            if dc:
                part = jnp.where((lane // 32) % 2 == 0, pltpu.roll(part, 96, 1), pltpu.roll(part, 32, 1))
            groups.append(part)
        both = jnp.concatenate(groups, axis=1)
        return both[0:1], both[1:2]

    classes = []
    for odd in range(2):
        for dc in range(2):
            stats = []
            for dz in range(odd, 8, 2):
                k = dz * 2 + dc
                if k == 0:
                    stats.append((peak, total))
                    continue
                stb[k].wait_recv()
                got = RSB[k]
                stats.append((got[0:1], got[1:2]))
            classes.append(reorder(*merge(stats), odd, dc))
    peak, total = merge(classes)

    for cp in me_y:
        cp.wait_recv()

    def facts():
        groups = []
        for dy in range(4):
            part = META[dy, 0, 0]
            for k in range(1, 4):
                part = part + pltpu.roll(META[dy, k // 2, k % 2], 32 * k, 1)
            groups.append(part)
        return jnp.concatenate(groups, axis=1)

    fact = facts()
    offset = (pipe * 16 + tensor) * VOC
    coefs, target, token = fact[2:3], fact[1:2], fact[0:1]
    inverse = 1.0 / total

    for i in range(5):
        rows = pl.ds(i * 128, 128)
        vocab = (offset + i * 128 + lax.broadcasted_iota(jnp.int32, (128, 1), 0)).astype(F32)
        hit = (target == vocab).astype(F32)
        grad = coefs * (jnp.exp(LT[rows, :] - peak) * inverse - hit)
        GS[rows, :] = grad.astype(BF16)
        turned = grad.T.astype(BF16)
        GT[:, :, :, :, i * 128 : (i + 1) * 128] = turned.reshape(4, 2, 2, ROWS, 128)
    gts = [
        send(GT.at[:, :, k, :, 0:VOC], GT.at[:, :, 1 - k, :, VOC : 2 * VOC], dev(dc=1)) for k in range(2)
    ]
    eh_s.wait_recv()
    ld_eh.wait()
    for cp in gts:
        cp.wait_recv()

    def partial(full, halves, base):
        def tile(n, _):
            at = pl.ds(align(n * QUART), QUART)
            got = jnp.dot(
                GT[...].reshape(TOK, 2 * VOC), EH[:, pl.ds(align(base + n * QUART), QUART)],
                preferred_element_type=F32,
            ).reshape(4, 2, 2, ROWS, QUART)
            full[..., at] = got[: full.shape[0]]
            halves[..., at] = got.astype(BF16)
            return 0

        lax.fori_loop(0, W // QUART, tile, 0)

    def block_of(dx):
        xx = (x + dx) % 4
        return (xx // 2 + zl) % 2, (xx % 2 + c) % 2

    partial(PA, SA, 0)
    ra = [send(SA.at[dy], RA.at[dy - 1], dev(dy=dy)) for dy in (1, 3, 2)]
    partial(PB, SB, W)
    rb = []
    for dx in (1, 3, 2):
        dz, dc = block_of(dx)
        rb.append(send(SB.at[:, dz, dc], RB.at[dx - 1], dev(dx=dx)))

    gat_c.relay(0, 1)
    gat_c.s1(2)
    gat_c.relay(1, 1)
    gat_c.s4(0)
    gat_c.relay(0, 2)
    gat_c.relay(1, 2)
    gat_c.s4(1)
    gat_c.s4(2)
    vv[2].wait_recv()
    value_step(3, dev(dy=2))
    for j in range(3):
        gat_c.s5(j)

    vocab = (offset + lax.broadcasted_iota(jnp.int32, (VOC, 1), 0)).astype(F32)
    LK = (token == vocab).astype(BF16)
    LT[...] = jnp.zeros_like(LT)
    normalizer = math.sqrt(D)
    outs = []
    for n in range(6):
        at = slice(n * PIECE, (n + 1) * PIECE)
        head = jnp.dot(GS[...], H[:, :, :, :, at].reshape(TOK, PIECE), preferred_element_type=F32)
        looked = jnp.dot(LK, C[:, :, :, :, at].reshape(TOK, PIECE), preferred_element_type=F32)
        if n >= 2:
            outs[n - 2].wait()
        GO[n % 2] = (head + normalizer * looked).astype(BF16)
        outs.append(load(GO.at[n % 2], ge.at[:, at], 4 + n))

    for cp in ra:
        cp.wait_recv()
    sum_a = PA[0]
    for k in range(3):
        sum_a += RA[k].astype(F32)
    PA[0] = sum_a
    SA2[...] = sum_a.astype(BF16)
    ra2 = []
    for dx in (1, 3, 2):
        dz, dc = block_of(dx)
        ra2.append(send(SA2.at[dz, dc], RA2.at[dx - 1], dev(dx=dx)))
    dz0, dc0 = block_of(0)
    for cp in rb:
        cp.wait_recv()
    sum_b = PB[:, dz0, dc0]
    for k in range(3):
        sum_b += RB[k].astype(F32)
    SB2[...] = sum_b.astype(BF16)
    rb2 = [send(SB2.at[dy], RB2.at[dy - 1], dev(dy=dy)) for dy in (1, 3, 2)]
    for cp in ra2:
        cp.wait_recv()
    fin_a = PA[0, dz0, dc0]
    for k in range(3):
        fin_a += RA2[k].astype(F32)
    ZS[0] = fin_a.astype(BF16).reshape(2, 16, W)
    for cp in rb2:
        cp.wait_recv()
    fin_b = sum_b[0]
    for k in range(3):
        fin_b += RB2[k].astype(F32)
    ZS[1] = fin_b.astype(BF16).reshape(2, 16, W)

    away = (x // 2 + zl) % 2
    zk = counter[0]
    counter[0] += 8

    def z_copy(k):
        zz = (z + away + 2 * k) % 8
        piece = zz // 2
        slot = away * 4 + k
        return pltpu.make_async_remote_copy(
            src_ref=ZS.at[piece // 2, piece % 2], dst_ref=ZR.at[slot], send_sem=ss.at[zk + k],
            recv_sem=rs.at[zk + slot], device_id=dev(dz=away + 2 * k), device_id_type=MESH,
        )

    for k in range(1, 4):
        z_copy(k).start()

    @pl.when(away == 1)
    def _():
        z_copy(0).start()

    gk = counter[0]
    counter[0] += 3
    ok = counter[0]
    counter[0] += 4

    def g_copy(k):
        return pltpu.make_async_remote_copy(
            src_ref=FZ.at[zh // 2, zh % 2], dst_ref=FZ.at[zh // 2, zh % 2], send_sem=ss.at[gk + k - 1],
            recv_sem=rs.at[gk + k - 1], device_id=dev(dz=2 * k), device_id_type=MESH,
        )

    tok_core = x % 2

    def o_copy(dx):
        xx = (x + dx) % 4
        return pltpu.make_async_remote_copy(
            src_ref=FZ, dst_ref=OUT.at[c], send_sem=ss.at[ok + dx], recv_sem=rs.at[ok + c],
            device_id=(xx * 4 + zh, zl * 8 + y * 2 + tok_core), device_id_type=MESH,
        )

    @pl.when(away == 0)
    def _():
        for slot in range(1, 8):
            pltpu.make_async_remote_copy(
                src_ref=ZR.at[slot], dst_ref=ZR.at[slot], send_sem=ss.at[zk], recv_sem=rs.at[zk + slot],
                device_id=dev(dz=1), device_id_type=MESH,
            ).wait_recv()
        ab, rh = zh // 2, zh % 2
        acc = ZS[ab, rh].astype(F32)
        for slot in range(1, 8):
            acc += ZR[slot].astype(F32)
        row = META[0, 0, dc0, 3:4, :]
        lanes = lax.broadcasted_iota(jnp.int32, (16, 128), 1)
        picks = lanes == lax.broadcasted_iota(jnp.int32, (16, 128), 0) + 16 * rh
        delta16 = jnp.sum(jnp.where(picks, row, 0.0), axis=1, keepdims=True)
        wide = vw[:, pl.ds(align(c * HALF + ab * W), W)].astype(F32)
        FZ[ab, rh] = (acc + delta16 * wide).astype(BF16)
        for k in range(1, 4):
            g_copy(k).start()
        for k in range(1, 4):
            piece = (zh - k + 4) % 4
            part = FZ.at[piece // 2, piece % 2]
            pltpu.make_async_remote_copy(
                src_ref=part, dst_ref=part, send_sem=ss.at[gk], recv_sem=rs.at[gk + k - 1],
                device_id=dev(dz=2), device_id_type=MESH,
            ).wait_recv()
        for dx in (1, 3, 2):
            o_copy(dx).start()

        @pl.when(tok_core == c)
        def _():
            local = pltpu.make_async_copy(FZ, OUT.at[c], xs.at[0])
            local.start()
            local.wait()

        @pl.when(tok_core != c)
        def _():
            o_copy(0).start()

    vv[3].wait_recv()
    gv[...] = VB[3] + VR[3]

    def o_wait(core):
        pltpu.make_async_remote_copy(
            src_ref=FZ, dst_ref=OUT.at[core], send_sem=ss.at[ok], recv_sem=rs.at[ok + core],
            device_id=dev(dx=1), device_id_type=MESH,
        ).wait_recv()

    home = (zl * 2 + c) == x
    o_wait(1 - c)

    @pl.when(jnp.logical_not(home))
    def _():
        o_wait(c)

    for cs in range(2):
        for ab in range(2):
            at = cs * HALF + ab * W
            for rh in range(2):
                gh[rh * 16 : (rh + 1) * 16, at : at + W] = OUT[cs, ab, rh]

    assert counter[0] <= SENDS, counter[0]
    for cp in started:
        cp.wait_send()
    for k in range(1, 4):
        z_copy(k).wait_send()

    @pl.when(away == 1)
    def _():
        z_copy(0).wait_send()

    @pl.when(away == 0)
    def _():
        for k in range(1, 4):
            g_copy(k).wait_send()
        for dx in (1, 3, 2):
            o_copy(dx).wait_send()

        @pl.when(tok_core != c)
        def _():
            o_copy(0).wait_send()

    for cp in outs[-2:]:
        cp.wait()


def local(hidden_states, embedding, token_ids, target_ids, coefficients, cotangent, value_weight, returns):
    vmem, anywhere = pl.BlockSpec(memory_space=pltpu.VMEM), pl.BlockSpec(memory_space=pl.ANY)
    V, dma = pltpu.VMEM, pltpu.SemaphoreType.DMA
    ge, gh, gv = pl.pallas_call(
        kernel,
        out_shape=(
            jax.ShapeDtypeStruct((VOC, D), BF16),
            jax.ShapeDtypeStruct((ROWS, D), BF16),
            jax.ShapeDtypeStruct((1, D), F32),
        ),
        in_specs=[anywhere, anywhere, vmem, vmem, vmem, anywhere, vmem, vmem],
        out_specs=(anywhere, vmem, vmem),
        scratch_shapes=[
            V((4, 2, 2, ROWS, D), BF16),
            V((4, 2, 2, ROWS, D), BF16),
            V((VOC, D), BF16),
            V((2 * VOC, HALF), BF16),
            V((VOC, TOK), F32),
            V((VOC, TOK), BF16),
            V((4, 2, 2, ROWS, 2 * VOC), BF16),
            V((1, 2, 2, ROWS, W), F32),
            V((4, 2, 2, ROWS, W), F32),
            V((4, 2, 2, ROWS, W), BF16),
            V((4, 2, 2, ROWS, W), BF16),
            V((3, 2, 2, ROWS, W), BF16),
            V((3, 4, ROWS, W), BF16),
            V((2, 2, ROWS, W), BF16),
            V((4, ROWS, W), BF16),
            V((3, ROWS, W), BF16),
            V((3, ROWS, W), BF16),
            V((2, 2, 16, W), BF16),
            V((8, 16, W), BF16),
            V((2, 2, 16, W), BF16),
            V((2, 2, 2, 16, W), BF16),
            V((4, 2, 2, 8, 128), F32),
            V((2, TOK), F32),
            V((16, 2, TOK), F32),
            V((2, TOK), F32),
            V((16, 2, TOK), F32),
            V((4, 1, D), F32),
            V((4, 1, D), F32),
            V((2, VOC, PIECE), BF16),
            dma((SENDS,)),
            dma((SENDS,)),
            dma((10,)),
            dma((1,)),
        ],
        compiler_params=pltpu.CompilerParams(
            collective_id=0, has_side_effects=True, vmem_limit_bytes=60 << 20
        ),
        name="policy_head",
    )(
        hidden_states, embedding, token_ids.reshape(1, ROWS), target_ids.reshape(1, ROWS),
        coefficients.reshape(1, ROWS), cotangent, value_weight.reshape(1, D), returns.reshape(1, ROWS),
    )
    return ge, gh, gv.reshape(D)


def solution(mesh):
    in_specs = (
        P("tensor", None),
        P(("pipe", "tensor"), None),
        P("tensor"),
        P("tensor"),
        P("tensor"),
        P("tensor", None),
        P(),
        P("tensor"),
    )
    out_specs = (P(("pipe", "tensor"), None), P("tensor", None), P())
    return jax.shard_map(local, mesh=mesh, in_specs=in_specs, out_specs=out_specs, check_vma=False)
```

```python
import math

import jax
import jax.numpy as jnp
from jax import lax
from jax.experimental import pallas as pl
from jax.experimental.pallas import tpu as pltpu
from jax.sharding import PartitionSpec as P

VALUE_SCALE = 0.5
MESH = pl.DeviceIdType.MESH
F32, BF16 = jnp.float32, jnp.bfloat16

ROWS = 32
TOK = 512
D = 4608
HALF = D // 2
PIECE = 768
QUART = PIECE // 2
VOC = 640
W = HALF // 2
SENDS = 224


def align(value, to=128):
    return pl.multiple_of(value, to)


def kernel(
    hs, emb, tid, tgt, coef, cot, vw, ret,
    ge, gh, gv,
    H, C, E, EH, LT, GS, GT, PA, PB, SA, SB, RA, RB, SA2, SB2, RA2, RB2,
    ZS, ZR, FZ, OUT, META, STA, RSA, STB, RSB, VB, VR, VW, LK,
    ss, rs, ls, xs,
):
    pipe, tensor = lax.axis_index("pipe"), lax.axis_index("tensor")
    x, zh = pipe // 4, pipe % 4
    zl, y, c = tensor // 8, (tensor // 2) % 4, tensor % 2
    z = 2 * zh + zl
    q = x % 2

    def dev(dx=0, dy=0, dz=0, dc=0):
        xx, yy, zz, cc = (x + dx) % 4, (y + dy) % 4, (z + dz + 8) % 8, (c + dc) % 2
        return xx * 4 + zz // 2, (zz % 2) * 8 + yy * 2 + cc

    pair = 1 - 2 * zl

    counter = [0]
    started = []

    def send(src, dst, target):
        k = counter[0]
        counter[0] += 1
        cp = pltpu.make_async_remote_copy(
            src_ref=src, dst_ref=dst, send_sem=ss.at[k], recv_sem=rs.at[k],
            device_id=target, device_id_type=MESH,
        )
        cp.start()
        started.append(cp)
        return cp

    def load(src, dst, k):
        cp = pltpu.make_async_copy(src, dst, ls.at[k])
        cp.start()
        return cp

    my_half = pl.ds(align(c * HALF), HALF)
    sib_half = pl.ds(align((1 - c) * HALF), HALF)
    ld_h = load(hs, H.at[0, 0, 0], 0)
    ld_e = load(emb, E, 1)
    ld_c = load(cot, C.at[0, 0, 0], 2)
    ld_eh = load(emb.at[:, my_half], EH.at[0:VOC], 3)

    plane = [(dx, dy) for dx in range(4) for dy in range(4) if (dx, dy) != (0, 0)]
    column = [(dz, dc) for dz in range(8) for dc in range(2) if (dz, dc) != (0, 0)]
    peers = [(dx, dy, 0, 0) for dx, dy in plane] + [(0, 0, dz, dc) for dz, dc in column]
    peers += [(dx, 0, 0, 1) for dx in (1, 2, 3)]
    bar = pltpu.get_barrier_semaphore()
    for peer in peers:
        pl.semaphore_signal(bar, inc=1, device_id=dev(*peer), device_id_type=MESH)

    META[0, 0, 0] = jnp.zeros((8, 128), F32)
    META[0, 0, 0, 0:1, 0:ROWS] = tid[...].astype(F32)
    META[0, 0, 0, 1:2, 0:ROWS] = tgt[...].astype(F32)
    META[0, 0, 0, 2:3, 0:ROWS] = coef[...].astype(F32)
    pl.semaphore_wait(bar, len(peers))

    def cols(half, j):
        return pl.ds(align(half * HALF + j * PIECE), PIECE)

    def quarter(half, j, k):
        return pl.ds(align(half * HALF + j * PIECE + k * QUART), QUART)

    class Gather:
        def __init__(self, X, by_z):
            self.X, self.by_z = X, by_z
            self.m = {}

        def again(self, key, part):
            pltpu.make_async_remote_copy(
                src_ref=part, dst_ref=part, send_sem=ss.at[self.m[key]], recv_sem=rs.at[self.m[key]],
                device_id=dev(dc=1), device_id_type=MESH,
            ).wait_recv()

        def begin(self):
            X, m = self.X, self.m
            order = sorted(range(3), key=lambda j: self.by_z[j])
            for j in order:
                if not self.by_z[j]:
                    self.zsend(j)
            for j in range(3):
                self.ysend(0, j)
                if j == 0:
                    m["s0"] = send(X.at[0, 0, 0], X.at[0, 0, 1], dev(dc=1))
            for j in order:
                if self.by_z[j]:
                    self.zsend(j)

        def zsend(self, j):
            X, m = self.X, self.m
            m["za", j] = send(X.at[0, 0, 0, :, cols(q, j)], X.at[0, 1, 0, :, cols(q, j)], dev(dz=1))
            m["zb", j] = send(X.at[0, 0, 0, :, cols(1 - q, j)], X.at[0, 1, 0, :, cols(1 - q, j)], dev(dz=-1))

        def ysend(self, dz, j):
            X, m = self.X, self.m
            for dy in (1, 3, 2):
                part = X.at[0, dz, 0, :, cols(q, j)]
                m["y", dz, dy, j] = send(part, X.at[dy, dz, 0, :, cols(q, j)], dev(dy=-dy))

        def s1(self, j):
            X, m = self.X, self.m
            m["za", j].wait_recv()
            if not self.by_z[j]:
                self.ysend(1, j)
            m["zb", j].wait_recv()
            for h, k in ((q, "sza"), (1 - q, "szb")):
                m[k, j] = send(X.at[0, 1, 0, :, cols(h, j)], X.at[0, 1, 1, :, cols(h, j)], dev(dc=1))

        def relay(self, dz, j):
            X, m = self.X, self.m
            for dy in (1, 2, 3):
                m["y", dz, dy, j].wait_recv()
            rows = pl.ds(1, 3)
            for k, dx in ((0, 1), (1, -1)):
                part = X.at[rows, dz, 0, :, quarter(q, j, k)]
                m["x", dz, k, j] = counter[0]
                send(part, part, dev(dx=dx))
            if self.by_z[j]:
                m["zc", j] = send(X.at[rows, 0, 0, :, cols(q, j)], X.at[rows, 1, 0, :, cols(q, j)], dev(dz=1))
            m["sy", dz, j] = send(
                X.at[rows, dz, 0, :, cols(q, j)], X.at[rows, dz, 1, :, cols(q, j)], dev(dc=1)
            )

        def s4(self, j):
            X, m = self.X, self.m
            rows = pl.ds(1, 3)
            for dz in range(1 if self.by_z[j] else 2):
                for k in range(2):
                    self.again(("x", dz, k, j), X.at[rows, dz, 0, :, quarter(1 - q, j, k)])
                part = cols(1 - q, j)
                if self.by_z[j]:
                    m["zd", j] = send(X.at[rows, 0, 0, :, part], X.at[rows, 1, 0, :, part], dev(dz=-1))
                m["sx", dz, j] = send(X.at[rows, dz, 0, :, part], X.at[rows, dz, 1, :, part], dev(dc=1))

        def s4z(self, j):
            X, m = self.X, self.m
            rows = pl.ds(1, 3)
            for key, back, h in (("zc", "sy", q), ("zd", "sx", 1 - q)):
                m[key, j].wait_recv()
                part = cols(h, j)
                m[back, 1, j] = send(X.at[rows, 1, 0, :, part], X.at[rows, 1, 1, :, part], dev(dc=1))

        def s5(self, j):
            m = self.m
            if j == 0:
                m["s0"].wait_recv()
            for k in ("sza", "szb"):
                m[k, j].wait_recv()
            for dz in range(2):
                m["sy", dz, j].wait_recv()
                m["sx", dz, j].wait_recv()

    gat_h, gat_c = Gather(H, (True, True, False)), Gather(C, (True, True, True))

    ld_h.wait()
    gat_h.begin()

    h_own = H[0, 0, 0].astype(F32)
    for k in range(D // 128):
        VW[:, k * 128 : (k + 1) * 128] = vw[k : k + 1, :].astype(F32)
    value_out = jnp.sum(h_own * VW[...], axis=1, keepdims=True)
    eye = lax.broadcasted_iota(jnp.int32, (ROWS, ROWS), 0) == lax.broadcasted_iota(jnp.int32, (ROWS, ROWS), 1)
    ret_col = jnp.sum(jnp.where(eye, jnp.broadcast_to(ret[...], (ROWS, ROWS)), 0.0), axis=1, keepdims=True)
    delta = VALUE_SCALE * (value_out - ret_col)
    META[0, 0, 0, 3:4, 0:ROWS] = jnp.sum(jnp.where(eye, delta, 0.0), axis=0, keepdims=True)
    VB[0] = jnp.sum(delta * h_own, axis=0, keepdims=True)
    me_s = send(META.at[0, 0, 0], META.at[0, 0, 1], dev(dc=1))
    vv = [send(VB.at[0], VR.at[0], dev(dc=1))]

    gat_h.s1(2)
    gat_h.relay(0, 0)
    ld_e.wait()
    eh_s = send(E.at[:, sib_half], EH.at[VOC : 2 * VOC], dev(dc=1))
    gat_h.s1(0)
    gat_h.relay(0, 1)
    gat_h.s1(1)
    gat_h.s4(0)
    gat_h.relay(0, 2)
    me_s.wait_recv()
    me_z = send(META.at[0, 0], META.at[0, 1], dev(dz=pair))
    gat_h.s4(1)
    gat_h.relay(1, 2)
    gat_h.s4z(0)
    me_z.wait_recv()
    me_y = [send(META.at[0], META.at[dy], dev(dy=-dy)) for dy in (1, 2, 3)]
    vv[0].wait_recv()

    def value_step(k, target):
        VB[k] = VB[k - 1] + VR[k - 1]
        vv.append(send(VB.at[k], VR.at[k], target))

    value_step(1, dev(dz=pair))
    gat_h.s5(0)

    def logits(j):
        def tile(n, _):
            total = jnp.zeros((VOC, 256), F32)
            for half in range(2):
                at = half * HALF + j * PIECE
                rows = H[pl.ds(2 * n, 2), :, :, :, at : at + PIECE].reshape(256, PIECE)
                total += lax.dot_general(
                    E[:, at : at + PIECE], rows, (((1,), (1,)), ((), ())), preferred_element_type=F32
                )
            where = (slice(None), pl.ds(align(n * 256, 256), 256))
            LT[where] = total if j == 0 else LT[where] + total
            return 0

        lax.fori_loop(0, 2, tile, 0)

    logits(0)
    gat_h.s4z(1)
    ld_c.wait()
    gat_c.begin()
    gat_h.s5(1)
    logits(1)
    gat_h.s4(2)
    vv[1].wait_recv()
    value_step(2, dev(dy=1 - 2 * (y % 2)))
    gat_h.s5(2)
    logits(2)

    peak = jnp.max(LT[...], axis=0, keepdims=True)
    total = jnp.sum(jnp.exp(LT[...] - peak), axis=0, keepdims=True)
    STA[0:1] = peak
    STA[1:2] = total
    sta = {}
    for dx, dy in plane:
        back = (-dx % 4) * 4 + (-dy % 4)
        sta[back] = send(STA, RSA.at[back], dev(dx=dx, dy=dy))

    def merge(stats):
        peaks = stats[0][0]
        for p, _ in stats[1:]:
            peaks = jnp.maximum(peaks, p)
        sums = sum(s * jnp.exp(p - peaks) for p, s in stats)
        return peaks, sums

    gat_c.s1(0)
    gat_c.relay(0, 0)

    stats = [(peak, total)]
    for dx, dy in plane:
        k = dx * 4 + dy
        sta[k].wait_recv()
        got = RSA[k]
        if dy:
            got = jnp.concatenate([got[:, 128 * (4 - dy) :], got[:, : 128 * (4 - dy)]], axis=1)
        stats.append((got[0:1], got[1:2]))
    peak, total = merge(stats)
    STB[0:1] = peak
    STB[1:2] = total
    stb = {}
    for dz, dc in column:
        back = (-dz % 8) * 2 + dc
        stb[back] = send(STB, RSB.at[back], dev(dz=dz, dc=dc))

    gat_c.s1(1)
    gat_c.relay(0, 1)
    gat_c.s4(0)

    lane = lax.broadcasted_iota(jnp.int32, (2, 128), 1)

    def reorder(p, s, odd, dc):
        both = jnp.concatenate([p, s], axis=0)
        groups = []
        for g in range(4):
            part = both[:, 128 * g : 128 * (g + 1)]
            if odd:
                part = pltpu.roll(part, 64, 1)
            if dc:
                part = jnp.where((lane // 32) % 2 == 0, pltpu.roll(part, 96, 1), pltpu.roll(part, 32, 1))
            groups.append(part)
        both = jnp.concatenate(groups, axis=1)
        return both[0:1], both[1:2]

    classes = []
    for odd in range(2):
        for dc in range(2):
            stats = []
            for dz in range(odd, 8, 2):
                k = dz * 2 + dc
                if k == 0:
                    stats.append((peak, total))
                    continue
                stb[k].wait_recv()
                got = RSB[k]
                stats.append((got[0:1], got[1:2]))
            classes.append(reorder(*merge(stats), odd, dc))
    peak, total = merge(classes)

    for cp in me_y:
        cp.wait_recv()

    def facts():
        groups = []
        for dy in range(4):
            part = META[dy, 0, 0]
            for k in range(1, 4):
                part = part + pltpu.roll(META[dy, k // 2, k % 2], 32 * k, 1)
            groups.append(part)
        return jnp.concatenate(groups, axis=1)

    fact = facts()
    offset = (pipe * 16 + tensor) * VOC
    coefs, target, token = fact[2:3], fact[1:2], fact[0:1]
    inverse = 1.0 / total

    for i in range(5):
        rows = pl.ds(i * 128, 128)
        vocab = (offset + i * 128 + lax.broadcasted_iota(jnp.int32, (128, 1), 0)).astype(F32)
        hit = (target == vocab).astype(F32)
        grad = coefs * (jnp.exp(LT[rows, :] - peak) * inverse - hit)
        GS[rows, :] = grad.astype(BF16)
        turned = grad.T.astype(BF16)
        GT[:, :, :, :, i * 128 : (i + 1) * 128] = turned.reshape(4, 2, 2, ROWS, 128)
    gts = [
        send(GT.at[:, :, k, :, 0:VOC], GT.at[:, :, 1 - k, :, VOC : 2 * VOC], dev(dc=1)) for k in range(2)
    ]
    gat_c.s1(2)
    gat_c.relay(0, 2)
    eh_s.wait_recv()
    ld_eh.wait()
    for cp in gts:
        cp.wait_recv()

    def block_of(dx):
        xx = (x + dx) % 4
        return (xx // 2 + zl) % 2, (xx % 2 + c) % 2

    dz0, dc0 = block_of(0)
    away = (x // 2 + zl) % 2
    tok_core = x % 2
    ra, rb, ra2, rb2, zk, gk, ok = {}, {}, {}, {}, {}, {}, {}

    def partial(k, base):
        at = pl.ds(base + k * QUART, QUART)
        return jnp.dot(
            GT[...].reshape(TOK, 2 * VOC), EH[:, at], preferred_element_type=F32
        ).reshape(4, 2, 2, ROWS, QUART)

    def r1(k):
        got = partial(k, 0)
        PA[k] = got[0]
        SA[k] = got.astype(BF16)
        ra[k] = [send(SA.at[k, dy], RA.at[k, dy - 1], dev(dy=dy)) for dy in (1, 3, 2)]
        got = partial(k, W)
        PB[k] = got
        SB[k] = got.astype(BF16)
        rb[k] = []
        for dx in (1, 3, 2):
            dz, dc = block_of(dx)
            rb[k].append(send(SB.at[k, :, dz, dc], RB.at[k, dx - 1], dev(dx=dx)))

    def r2(k):
        for cp in ra[k]:
            cp.wait_recv()
        total = PA[k]
        for i in range(3):
            total += RA[k, i].astype(F32)
        PA[k] = total
        SA2[k] = total.astype(BF16)
        ra2[k] = []
        for dx in (1, 3, 2):
            dz, dc = block_of(dx)
            ra2[k].append(send(SA2.at[k, dz, dc], RA2.at[k, dx - 1], dev(dx=dx)))
        for cp in rb[k]:
            cp.wait_recv()
        total = PB[k, :, dz0, dc0]
        for i in range(3):
            total += RB[k, i].astype(F32)
        PB[k, 0, 0, 0] = total[0]
        SB2[k] = total.astype(BF16)
        rb2[k] = [send(SB2.at[k, dy], RB2.at[k, dy - 1], dev(dy=dy)) for dy in (1, 3, 2)]

    def z_copy(k, i):
        zz = (z + away + 2 * i) % 8
        piece = zz // 2
        slot = away * 4 + i
        return pltpu.make_async_remote_copy(
            src_ref=ZS.at[k, piece // 2, piece % 2], dst_ref=ZR.at[k, slot], send_sem=ss.at[zk[k] + i],
            recv_sem=rs.at[zk[k] + slot], device_id=dev(dz=away + 2 * i), device_id_type=MESH,
        )

    def r3(k):
        for cp in ra2[k]:
            cp.wait_recv()
        total = PA[k, dz0, dc0]
        for i in range(3):
            total += RA2[k, i].astype(F32)
        ZS[k, 0] = total.astype(BF16).reshape(2, 16, QUART)
        for cp in rb2[k]:
            cp.wait_recv()
        total = PB[k, 0, 0, 0]
        for i in range(3):
            total += RB2[k, i].astype(F32)
        ZS[k, 1] = total.astype(BF16).reshape(2, 16, QUART)
        zk[k], gk[k], ok[k] = counter[0], counter[0] + 8, counter[0] + 11
        counter[0] += 15
        for i in range(1, 4):
            z_copy(k, i).start()

        @pl.when(away == 1)
        def _():
            z_copy(k, 0).start()

    def g_copy(k, i):
        part = FZ.at[k, zh // 2, zh % 2]
        return pltpu.make_async_remote_copy(
            src_ref=part, dst_ref=part, send_sem=ss.at[gk[k] + i - 1],
            recv_sem=rs.at[gk[k] + i - 1], device_id=dev(dz=2 * i), device_id_type=MESH,
        )

    def r4(k):
        @pl.when(away == 0)
        def _():
            for slot in range(1, 8):
                pltpu.make_async_remote_copy(
                    src_ref=ZR.at[k, slot], dst_ref=ZR.at[k, slot], send_sem=ss.at[zk[k]],
                    recv_sem=rs.at[zk[k] + slot], device_id=dev(dz=1), device_id_type=MESH,
                ).wait_recv()
            ab, rh = zh // 2, zh % 2
            acc = ZS[k, ab, rh].astype(F32)
            for slot in range(1, 8):
                acc += ZR[k, slot].astype(F32)
            row = META[0, 0, dc0, 3:4, :]
            lanes = lax.broadcasted_iota(jnp.int32, (16, 128), 1)
            picks = lanes == lax.broadcasted_iota(jnp.int32, (16, 128), 0) + 16 * rh
            delta16 = jnp.sum(jnp.where(picks, row, 0.0), axis=1, keepdims=True)
            wide = VW[:, pl.ds(align(c * HALF + ab * W + k * QUART), QUART)]
            FZ[k, ab, rh] = (acc + delta16 * wide).astype(BF16)
            for i in range(1, 4):
                g_copy(k, i).start()

    def o_copy(k, dx):
        xx = (x + dx) % 4
        return pltpu.make_async_remote_copy(
            src_ref=FZ.at[k], dst_ref=OUT.at[k, c], send_sem=ss.at[ok[k] + dx], recv_sem=rs.at[ok[k] + c],
            device_id=(xx * 4 + zh, zl * 8 + y * 2 + tok_core), device_id_type=MESH,
        )

    def r5(k):
        @pl.when(away == 0)
        def _():
            for i in range(1, 4):
                piece = (zh - i + 4) % 4
                part = FZ.at[k, piece // 2, piece % 2]
                pltpu.make_async_remote_copy(
                    src_ref=part, dst_ref=part, send_sem=ss.at[gk[k]], recv_sem=rs.at[gk[k] + i - 1],
                    device_id=dev(dz=2), device_id_type=MESH,
                ).wait_recv()
            for dx in (1, 3, 2):
                o_copy(k, dx).start()

            @pl.when(tok_core == c)
            def _():
                local = pltpu.make_async_copy(FZ.at[k], OUT.at[k, c], xs.at[k])
                local.start()
                local.wait()

            @pl.when(tok_core != c)
            def _():
                o_copy(k, 0).start()

    home = (zl * 2 + c) == x

    def r6(k):
        def o_wait(core):
            pltpu.make_async_remote_copy(
                src_ref=FZ.at[k], dst_ref=OUT.at[k, core], send_sem=ss.at[ok[k]], recv_sem=rs.at[ok[k] + core],
                device_id=dev(dx=1), device_id_type=MESH,
            ).wait_recv()

        o_wait(1 - c)

        @pl.when(jnp.logical_not(home))
        def _():
            o_wait(c)

        for cs in range(2):
            for ab in range(2):
                at = cs * HALF + ab * W + k * QUART
                for rh in range(2):
                    gh[rh * 16 : (rh + 1) * 16, at : at + QUART] = OUT[k, cs, ab, rh]

    vocab = (offset + lax.broadcasted_iota(jnp.int32, (VOC, 1), 0)).astype(F32)
    LK[...] = (token == vocab).astype(BF16)
    normalizer = math.sqrt(D)

    def embed(n):
        at = slice(n * PIECE, (n + 1) * PIECE)
        head = jnp.dot(GS[...], H[:, :, :, :, at].reshape(TOK, PIECE), preferred_element_type=F32)
        looked = jnp.dot(LK[...], C[:, :, :, :, at].reshape(TOK, PIECE), preferred_element_type=F32)
        ge[:, at] = (head + normalizer * looked).astype(BF16)

    r1(0)
    gat_c.s4(1)
    r1(1)
    gat_c.s4(2)
    r1(2)
    gat_c.s4z(0)
    vv[2].wait_recv()
    value_step(3, dev(dy=2))
    gat_c.s4z(1)
    gat_c.s5(0)
    embed(0)
    embed(3)
    r2(0)
    gat_c.s4z(2)
    gat_c.s5(1)
    embed(1)
    r2(1)
    r3(0)
    embed(4)
    gat_c.s5(2)
    r2(2)
    r3(1)
    r4(0)
    embed(2)
    r3(2)
    r4(1)
    r5(0)
    embed(5)
    r4(2)
    r5(1)
    r5(2)

    vv[3].wait_recv()
    for k in range(D // 128):
        at = slice(k * 128, (k + 1) * 128)
        gv[k : k + 1, :] = VB[3, :, at] + VR[3, :, at]

    for k in range(3):
        r6(k)

    assert counter[0] <= SENDS, counter[0]
    for cp in started:
        cp.wait_send()
    for k in range(3):
        for i in range(1, 4):
            z_copy(k, i).wait_send()

    @pl.when(away == 1)
    def _():
        for k in range(3):
            z_copy(k, 0).wait_send()

    @pl.when(away == 0)
    def _():
        for k in range(3):
            for i in range(1, 4):
                g_copy(k, i).wait_send()
            for dx in (1, 3, 2):
                o_copy(k, dx).wait_send()

        @pl.when(tok_core != c)
        def _():
            for k in range(3):
                o_copy(k, 0).wait_send()


def local(hidden_states, embedding, token_ids, target_ids, coefficients, cotangent, value_weight, returns):
    vmem, anywhere = pl.BlockSpec(memory_space=pltpu.VMEM), pl.BlockSpec(memory_space=pl.ANY)
    V, dma = pltpu.VMEM, pltpu.SemaphoreType.DMA
    ge, gh, gv = pl.pallas_call(
        kernel,
        out_shape=(
            pltpu.VMEM((VOC, D), BF16),
            pltpu.VMEM((ROWS, D), BF16),
            pltpu.VMEM((D // 128, 128), F32),
        ),
        in_specs=[anywhere, anywhere, vmem, vmem, vmem, anywhere, vmem, vmem],
        out_specs=(vmem, vmem, vmem),
        scratch_shapes=[
            V((4, 2, 2, ROWS, D), BF16),
            V((4, 2, 2, ROWS, D), BF16),
            V((VOC, D), BF16),
            V((2 * VOC, HALF), BF16),
            V((VOC, TOK), F32),
            V((VOC, TOK), BF16),
            V((4, 2, 2, ROWS, 2 * VOC), BF16),
            V((3, 2, 2, ROWS, QUART), F32),
            V((3, 4, 2, 2, ROWS, QUART), F32),
            V((3, 4, 2, 2, ROWS, QUART), BF16),
            V((3, 4, 2, 2, ROWS, QUART), BF16),
            V((3, 3, 2, 2, ROWS, QUART), BF16),
            V((3, 3, 4, ROWS, QUART), BF16),
            V((3, 2, 2, ROWS, QUART), BF16),
            V((3, 4, ROWS, QUART), BF16),
            V((3, 3, ROWS, QUART), BF16),
            V((3, 3, ROWS, QUART), BF16),
            V((3, 2, 2, 16, QUART), BF16),
            V((3, 8, 16, QUART), BF16),
            V((3, 2, 2, 16, QUART), BF16),
            V((3, 2, 2, 2, 16, QUART), BF16),
            V((4, 2, 2, 8, 128), F32),
            V((2, TOK), F32),
            V((16, 2, TOK), F32),
            V((2, TOK), F32),
            V((16, 2, TOK), F32),
            V((4, 1, D), F32),
            V((4, 1, D), F32),
            V((1, D), F32),
            V((VOC, TOK), BF16),
            dma((SENDS,)),
            dma((SENDS,)),
            dma((10,)),
            dma((3,)),
        ],
        compiler_params=pltpu.CompilerParams(
            collective_id=0, has_side_effects=True, vmem_limit_bytes=50 << 20
        ),
        name="policy_head",
    )(
        hidden_states, embedding, token_ids.reshape(1, ROWS), target_ids.reshape(1, ROWS),
        coefficients.reshape(1, ROWS), cotangent, value_weight.reshape(D // 128, 128), returns.reshape(1, ROWS),
    )
    return ge, gh, gv.reshape(D)


def solution(mesh):
    in_specs = (
        P("tensor", None),
        P(("pipe", "tensor"), None),
        P("tensor"),
        P("tensor"),
        P("tensor"),
        P("tensor", None),
        P(),
        P("tensor"),
    )
    out_specs = (P(("pipe", "tensor"), None), P("tensor", None), P())
    return jax.shard_map(local, mesh=mesh, in_specs=in_specs, out_specs=out_specs, check_vma=False)
```

```python
import math

import jax
import jax.numpy as jnp
from jax import lax
from jax.experimental import pallas as pl
from jax.experimental.pallas import tpu as pltpu
from jax.sharding import PartitionSpec as P

VALUE_SCALE = 0.5
MESH = pl.DeviceIdType.MESH
F32, BF16 = jnp.float32, jnp.bfloat16

ROWS = 32
TOK = 512
D = 4608
HALF = D // 2
PIECE = 768
QUART = PIECE // 2
VOC = 640
W = HALF // 2
SENDS = 256


def align(value, to=128):
    return pl.multiple_of(value, to)


def kernel(
    hs, emb, tid, tgt, coef, cot, vw, ret,
    ge, gh, gv,
    H, C, E, EH, LT, GS, GT, PA, PB, SA, SB, RA, RB, SA2, SB2, RA2, RB2,
    ZS, ZR, FZ, OUT, META, STA, RSA, STB, RSB, VB, VR, VW, LK,
    ss, rs, ls,
):
    pipe, tensor = lax.axis_index("pipe"), lax.axis_index("tensor")
    x, zh = pipe // 4, pipe % 4
    zl, y, c = tensor // 8, (tensor // 2) % 4, tensor % 2
    z = 2 * zh + zl
    q = x % 2

    def dev(dx=0, dy=0, dz=0, dc=0):
        xx, yy, zz, cc = (x + dx) % 4, (y + dy) % 4, (z + dz + 8) % 8, (c + dc) % 2
        return xx * 4 + zz // 2, (zz % 2) * 8 + yy * 2 + cc

    pair = 1 - 2 * zl

    counter = [0]
    started = []

    def send(src, dst, target):
        k = counter[0]
        counter[0] += 1
        cp = pltpu.make_async_remote_copy(
            src_ref=src, dst_ref=dst, send_sem=ss.at[k], recv_sem=rs.at[k],
            device_id=target, device_id_type=MESH,
        )
        cp.start()
        started.append(cp)
        return cp

    gone = set()

    def left(cp):
        if id(cp) not in gone:
            gone.add(id(cp))
            cp.wait_send()

    def flush(first=None):
        for cp in started[:first]:
            left(cp)

    def load(src, dst, k):
        cp = pltpu.make_async_copy(src, dst, ls.at[k])
        cp.start()
        return cp

    my_half = pl.ds(align(c * HALF), HALF)
    sib_half = pl.ds(align((1 - c) * HALF), HALF)
    ld_h = load(hs, H.at[0, 0, 0], 0)
    ld_e = load(emb, E, 1)
    ld_c = load(cot, C.at[0, 0, 0], 2)
    ld_eh = load(emb.at[:, my_half], EH.at[0:VOC], 3)

    plane = [(dx, dy) for dx in range(4) for dy in range(4) if (dx, dy) != (0, 0)]
    column = [(dz, dc) for dz in range(8) for dc in range(2) if (dz, dc) != (0, 0)]
    peers = [(d, 0, 0, 0) for d in (1, 2, 3)] + [(0, d, 0, 0) for d in (1, 2, 3)]
    peers += [(0, 0, d, 0) for d in range(1, 8)] + [(0, 0, 0, 1)]
    bar = pltpu.get_barrier_semaphore()
    for peer in peers:
        pl.semaphore_signal(bar, inc=1, device_id=dev(*peer), device_id_type=MESH)

    META[0, 0, 0] = jnp.zeros((8, 128), F32)
    META[0, 0, 0, 0:1, 0:ROWS] = tid[...].astype(F32)
    META[0, 0, 0, 1:2, 0:ROWS] = tgt[...].astype(F32)
    META[0, 0, 0, 2:3, 0:ROWS] = coef[...].astype(F32)
    pl.semaphore_wait(bar, len(peers))

    def cols(half, j):
        return pl.ds(align(half * HALF + j * PIECE), PIECE)

    def quarter(half, j, k):
        return pl.ds(align(half * HALF + j * PIECE + k * QUART), QUART)

    class Gather:
        def __init__(self, X, by_z):
            self.X, self.by_z = X, by_z
            self.m = {}

        def again(self, key, part):
            pltpu.make_async_remote_copy(
                src_ref=part, dst_ref=part, send_sem=ss.at[self.m[key]], recv_sem=rs.at[self.m[key]],
                device_id=dev(dc=1), device_id_type=MESH,
            ).wait_recv()

        def own(self):
            self.m["s0"] = send(self.X.at[0, 0, 0], self.X.at[0, 0, 1], dev(dc=1))

        def gate(self, j):
            for dz in range(1 if self.by_z[j] else 2):
                for dy in (1, 3, 2):
                    left(self.m["y", dz, dy, j])

        def zsend(self, j):
            X, m = self.X, self.m
            m["za", j] = send(X.at[0, 0, 0, :, cols(q, j)], X.at[0, 1, 0, :, cols(q, j)], dev(dz=1))
            m["zb", j] = send(X.at[0, 0, 0, :, cols(1 - q, j)], X.at[0, 1, 0, :, cols(1 - q, j)], dev(dz=-1))

        def ysend(self, dz, j):
            X, m = self.X, self.m
            for dy in (1, 3, 2):
                part = X.at[0, dz, 0, :, cols(q, j)]
                m["y", dz, dy, j] = send(part, X.at[dy, dz, 0, :, cols(q, j)], dev(dy=-dy))

        def s0(self, j):
            self.m["za", j].wait_recv()
            self.ysend(1, j)

        def s1(self, j):
            X, m = self.X, self.m
            if self.by_z[j]:
                m["za", j].wait_recv()
            m["zb", j].wait_recv()
            for h, k in ((q, "sza"), (1 - q, "szb")):
                m[k, j] = send(X.at[0, 1, 0, :, cols(h, j)], X.at[0, 1, 1, :, cols(h, j)], dev(dc=1))

        def relay(self, dz, j):
            X, m = self.X, self.m
            for dy in (1, 2, 3):
                m["y", dz, dy, j].wait_recv()
            rows = pl.ds(1, 3)
            for k, dx in ((0, 1), (1, -1)):
                part = X.at[rows, dz, 0, :, quarter(q, j, k)]
                m["x", dz, k, j] = counter[0]
                send(part, part, dev(dx=dx))
            if self.by_z[j]:
                m["zc", j] = send(X.at[rows, 0, 0, :, cols(q, j)], X.at[rows, 1, 0, :, cols(q, j)], dev(dz=1))
            m["sy", dz, j] = send(
                X.at[rows, dz, 0, :, cols(q, j)], X.at[rows, dz, 1, :, cols(q, j)], dev(dc=1)
            )

        def s4(self, j):
            X, m = self.X, self.m
            rows = pl.ds(1, 3)
            for dz in range(1 if self.by_z[j] else 2):
                for k in range(2):
                    self.again(("x", dz, k, j), X.at[rows, dz, 0, :, quarter(1 - q, j, k)])
                part = cols(1 - q, j)
                if self.by_z[j]:
                    m["zd", j] = send(X.at[rows, 0, 0, :, part], X.at[rows, 1, 0, :, part], dev(dz=-1))
                m["sx", dz, j] = send(X.at[rows, dz, 0, :, part], X.at[rows, dz, 1, :, part], dev(dc=1))

        def s4z(self, j):
            X, m = self.X, self.m
            rows = pl.ds(1, 3)
            for key, back, h in (("zc", "sy", q), ("zd", "sx", 1 - q)):
                m[key, j].wait_recv()
                part = cols(h, j)
                m[back, 1, j] = send(X.at[rows, 1, 0, :, part], X.at[rows, 1, 1, :, part], dev(dc=1))

        def s5(self, j):
            m = self.m
            if j == 0:
                m["s0"].wait_recv()
            for k in ("sza", "szb"):
                m[k, j].wait_recv()
            for dz in range(2):
                m["sy", dz, j].wait_recv()
                m["sx", dz, j].wait_recv()

    gat_h, gat_c = Gather(H, (True, False, False)), Gather(C, (True, True, True))

    ld_h.wait()
    gat_h.zsend(1)
    gat_h.ysend(0, 0)
    gat_h.zsend(2)
    gat_h.zsend(0)
    gat_h.own()
    eh_s = send(emb.at[:, sib_half], EH.at[VOC : 2 * VOC], dev(dc=1))

    h_own = H[0, 0, 0].astype(F32)
    for k in range(D // 128):
        VW[:, k * 128 : (k + 1) * 128] = vw[k : k + 1, :].astype(F32)
    value_out = jnp.sum(h_own * VW[...], axis=1, keepdims=True)
    eye = lax.broadcasted_iota(jnp.int32, (ROWS, ROWS), 0) == lax.broadcasted_iota(jnp.int32, (ROWS, ROWS), 1)
    ret_col = jnp.sum(jnp.where(eye, jnp.broadcast_to(ret[...], (ROWS, ROWS)), 0.0), axis=1, keepdims=True)
    delta = VALUE_SCALE * (value_out - ret_col)
    META[0, 0, 0, 3:4, 0:ROWS] = jnp.sum(jnp.where(eye, delta, 0.0), axis=0, keepdims=True)
    VB[0] = jnp.sum(delta * h_own, axis=0, keepdims=True)
    me_s = send(META.at[0, 0, 0], META.at[0, 0, 1], dev(dc=1))
    vv = [send(VB.at[0], VR.at[0], dev(dc=1))]

    gat_h.gate(0)
    gat_h.ysend(0, 1)
    gat_h.s0(1)
    gat_h.relay(0, 0)
    gat_h.s1(1)
    gat_h.gate(1)
    gat_h.ysend(0, 2)
    gat_h.s0(2)
    gat_h.relay(0, 1)
    gat_h.relay(1, 1)
    gat_h.s4(0)
    gat_h.s1(0)
    gat_h.s1(2)
    me_s.wait_recv()
    me_z = send(META.at[0, 0], META.at[0, 1], dev(dz=pair))
    gat_h.relay(0, 2)
    gat_h.s4(1)
    gat_h.relay(1, 2)
    ld_c.wait()
    gat_c.ysend(0, 0)
    gat_h.s4z(0)
    me_z.wait_recv()
    me_y = [send(META.at[0], META.at[dy], dev(dy=-dy)) for dy in (1, 2, 3)]
    vv[0].wait_recv()

    def value_step(k, target):
        VB[k] = VB[k - 1] + VR[k - 1]
        vv.append(send(VB.at[k], VR.at[k], target))

    value_step(1, dev(dz=pair))
    gat_h.s5(0)

    def logits(j):
        def tile(n, _):
            total = jnp.zeros((VOC, 256), F32)
            for half in range(2):
                at = half * HALF + j * PIECE
                rows = H[pl.ds(2 * n, 2), :, :, :, at : at + PIECE].reshape(256, PIECE)
                total += lax.dot_general(
                    E[:, at : at + PIECE], rows, (((1,), (1,)), ((), ())), preferred_element_type=F32
                )
            where = (slice(None), pl.ds(align(n * 256, 256), 256))
            LT[where] = total if j == 0 else LT[where] + total
            return 0

        lax.fori_loop(0, 2, tile, 0)

    ld_e.wait()
    logits(0)
    gat_h.s5(1)
    logits(1)
    gat_h.s4(2)
    vv[1].wait_recv()
    value_step(2, dev(dy=1 - 2 * (y % 2)))
    gat_c.gate(0)
    gat_c.ysend(0, 1)
    gat_c.zsend(0)
    gat_h.s5(2)
    logits(2)

    peak = jnp.max(LT[...], axis=0, keepdims=True)
    total = jnp.sum(jnp.exp(LT[...] - peak), axis=0, keepdims=True)
    STA[0:1] = peak
    STA[1:2] = total
    before_stats = len(started)
    sta = {}
    for dx, dy in plane:
        back = (-dx % 4) * 4 + (-dy % 4)
        sta[back] = send(STA, RSA.at[back], dev(dx=dx, dy=dy))

    def merge(stats):
        peaks = stats[0][0]
        for p, _ in stats[1:]:
            peaks = jnp.maximum(peaks, p)
        sums = sum(s * jnp.exp(p - peaks) for p, s in stats)
        return peaks, sums

    flush(before_stats)
    gat_c.ysend(0, 2)
    gat_c.relay(0, 0)
    gat_c.own()

    stats = [(peak, total)]
    for dx, dy in plane:
        k = dx * 4 + dy
        sta[k].wait_recv()
        got = RSA[k]
        if dy:
            got = jnp.concatenate([got[:, 128 * (4 - dy) :], got[:, : 128 * (4 - dy)]], axis=1)
        stats.append((got[0:1], got[1:2]))
    peak, total = merge(stats)
    STB[0:1] = peak
    STB[1:2] = total
    stb = {}
    for dz, dc in column:
        back = (-dz % 8) * 2 + dc
        stb[back] = send(STB, RSB.at[back], dev(dz=dz, dc=dc))

    gat_c.s1(0)
    gat_c.relay(0, 1)
    gat_c.zsend(1)
    gat_c.zsend(2)
    gat_c.s4(0)

    lane = lax.broadcasted_iota(jnp.int32, (2, 128), 1)

    def reorder(p, s, odd, dc):
        both = jnp.concatenate([p, s], axis=0)
        groups = []
        for g in range(4):
            part = both[:, 128 * g : 128 * (g + 1)]
            if odd:
                part = pltpu.roll(part, 64, 1)
            if dc:
                part = jnp.where((lane // 32) % 2 == 0, pltpu.roll(part, 96, 1), pltpu.roll(part, 32, 1))
            groups.append(part)
        both = jnp.concatenate(groups, axis=1)
        return both[0:1], both[1:2]

    classes = []
    for odd in range(2):
        for dc in range(2):
            stats = []
            for dz in range(odd, 8, 2):
                k = dz * 2 + dc
                if k == 0:
                    stats.append((peak, total))
                    continue
                stb[k].wait_recv()
                got = RSB[k]
                stats.append((got[0:1], got[1:2]))
            classes.append(reorder(*merge(stats), odd, dc))
    peak, total = merge(classes)

    for cp in me_y:
        cp.wait_recv()

    def facts():
        groups = []
        for dy in range(4):
            part = META[dy, 0, 0]
            for k in range(1, 4):
                part = part + pltpu.roll(META[dy, k // 2, k % 2], 32 * k, 1)
            groups.append(part)
        return jnp.concatenate(groups, axis=1)

    fact = facts()
    offset = (pipe * 16 + tensor) * VOC
    coefs, target, token = fact[2:3], fact[1:2], fact[0:1]
    inverse = 1.0 / total

    for i in range(5):
        rows = pl.ds(i * 128, 128)
        vocab = (offset + i * 128 + lax.broadcasted_iota(jnp.int32, (128, 1), 0)).astype(F32)
        hit = (target == vocab).astype(F32)
        grad = coefs * (jnp.exp(LT[rows, :] - peak) * inverse - hit)
        GS[rows, :] = grad.astype(BF16)
        turned = grad.T.astype(BF16)
        GT[:, :, :, :, i * 128 : (i + 1) * 128] = turned.reshape(4, 2, 2, ROWS, 128)
    gts = [
        send(GT.at[:, :, k, :, 0:VOC], GT.at[:, :, 1 - k, :, VOC : 2 * VOC], dev(dc=1)) for k in range(2)
    ]
    gat_c.s1(1)
    gat_c.s1(2)
    gat_c.relay(0, 2)
    eh_s.wait_recv()
    ld_eh.wait()
    for cp in gts:
        cp.wait_recv()

    def block_of(dx):
        xx = (x + dx) % 4
        return (xx // 2 + zl) % 2, (xx % 2 + c) % 2

    dz0, dc0 = block_of(0)
    away = (x // 2 + zl) % 2
    tok_core = x % 2
    ra, rb, ra2, rb2, zk, gk = {}, {}, {}, {}, {}, {}
    others = [(dx, i) for dx in (1, 3, 2, 0) for i in (1, 3, 2, 0) if (dx, i) != (0, 0)]

    def partial(k, base):
        at = pl.ds(base + k * QUART, QUART)
        return jnp.dot(
            GT[...].reshape(TOK, 2 * VOC), EH[:, at], preferred_element_type=F32
        ).reshape(4, 2, 2, ROWS, QUART)

    def p1(k):
        got = partial(k, 0)
        PA[k] = got[0]
        SA[k] = got.astype(BF16)
        got = partial(k, W)
        PB[k] = got
        SB[k] = got.astype(BF16)

    def r1(k):
        if k:
            for cp in ra[k - 1]:
                left(cp)
        ra[k] = [send(SA.at[k, dy], RA.at[k, dy - 1], dev(dy=dy)) for dy in (1, 3, 2)]
        if k:
            for cp in rb[k - 1]:
                left(cp)
        rb[k] = []
        for dx in (1, 3, 2):
            dz, dc = block_of(dx)
            rb[k].append(send(SB.at[k, :, dz, dc], RB.at[k, dx - 1], dev(dx=dx)))

    def r2(k):
        for cp in ra[k]:
            cp.wait_recv()
        total = PA[k]
        for i in range(3):
            total += RA[k, i].astype(F32)
        PA[k] = total
        SA2[k] = total.astype(BF16)
        ra2[k] = []
        for dx in (1, 3, 2):
            dz, dc = block_of(dx)
            ra2[k].append(send(SA2.at[k, dz, dc], RA2.at[k, dx - 1], dev(dx=dx)))
        for cp in rb[k]:
            cp.wait_recv()
        total = PB[k, :, dz0, dc0]
        for i in range(3):
            total += RB[k, i].astype(F32)
        PB[k, 0, 0, 0] = total[0]
        SB2[k] = total.astype(BF16)
        rb2[k] = [send(SB2.at[k, dy], RB2.at[k, dy - 1], dev(dy=dy)) for dy in (1, 3, 2)]

    def z_copy(k, i):
        zz = (z + away + 2 * i) % 8
        piece = zz // 2
        slot = away * 4 + i
        return pltpu.make_async_remote_copy(
            src_ref=ZS.at[k, piece // 2, piece % 2], dst_ref=ZR.at[k, slot], send_sem=ss.at[zk[k] + i],
            recv_sem=rs.at[zk[k] + slot], device_id=dev(dz=away + 2 * i), device_id_type=MESH,
        )

    def r3(k):
        for cp in ra2[k]:
            cp.wait_recv()
        total = PA[k, dz0, dc0]
        for i in range(3):
            total += RA2[k, i].astype(F32)
        ZS[k, 0] = total.astype(BF16).reshape(2, 16, QUART)
        for cp in rb2[k]:
            cp.wait_recv()
        total = PB[k, 0, 0, 0]
        for i in range(3):
            total += RB2[k, i].astype(F32)
        ZS[k, 1] = total.astype(BF16).reshape(2, 16, QUART)
        zk[k], gk[k] = counter[0], counter[0] + 8
        counter[0] += 24
        for i in range(1, 4):
            z_copy(k, i).start()

        @pl.when(away == 1)
        def _():
            z_copy(k, 0).start()

    def o_copy(k, dx, i):
        part = FZ.at[k]
        return pltpu.make_async_remote_copy(
            src_ref=part, dst_ref=OUT.at[k, c, zh // 2, zh % 2], send_sem=ss.at[gk[k] + dx * 4 + i],
            recv_sem=rs.at[gk[k] + c * 4 + zh], device_id=dev(dx, 0, 2 * i, tok_core + c), device_id_type=MESH,
        )

    def r4(k):
        @pl.when(away == 0)
        def _():
            for slot in range(1, 8):
                pltpu.make_async_remote_copy(
                    src_ref=ZR.at[k, slot], dst_ref=ZR.at[k, slot], send_sem=ss.at[zk[k]],
                    recv_sem=rs.at[zk[k] + slot], device_id=dev(dz=1), device_id_type=MESH,
                ).wait_recv()
            ab, rh = zh // 2, zh % 2
            acc = ZS[k, ab, rh].astype(F32)
            for slot in range(1, 8):
                acc += ZR[k, slot].astype(F32)
            row = META[0, 0, dc0, 3:4, :]
            lanes = lax.broadcasted_iota(jnp.int32, (16, 128), 1)
            picks = lanes == lax.broadcasted_iota(jnp.int32, (16, 128), 0) + 16 * rh
            delta16 = jnp.sum(jnp.where(picks, row, 0.0), axis=1, keepdims=True)
            wide = VW[:, pl.ds(align(c * HALF + ab * W + k * QUART), QUART)]
            FZ[k] = (acc + delta16 * wide).astype(BF16)
            for dx, i in others:
                o_copy(k, dx, i).start()

            @pl.when(tok_core == c)
            def _():
                OUT[k, c, ab, rh] = FZ[k]

            @pl.when(tok_core != c)
            def _():
                o_copy(k, 0, 0).start()

    home = (zl * 2 + c) == x

    def r6(k):
        def o_wait(core, piece):
            pltpu.make_async_remote_copy(
                src_ref=FZ.at[k], dst_ref=OUT.at[k, core, piece // 2, piece % 2], send_sem=ss.at[gk[k]],
                recv_sem=rs.at[gk[k] + core * 4 + piece], device_id=dev(dx=1), device_id_type=MESH,
            ).wait_recv()

        for i in range(4):
            o_wait(1 - c, i)
        for i in range(1, 4):
            o_wait(c, (zh + i) % 4)

        @pl.when(jnp.logical_not(home))
        def _():
            o_wait(c, zh)

        for cs in range(2):
            for ab in range(2):
                at = cs * HALF + ab * W + k * QUART
                for rh in range(2):
                    gh[rh * 16 : (rh + 1) * 16, at : at + QUART] = OUT[k, cs, ab, rh]

    vocab = (offset + lax.broadcasted_iota(jnp.int32, (VOC, 1), 0)).astype(F32)
    LK[...] = (token == vocab).astype(BF16)
    normalizer = math.sqrt(D)

    def embed(n):
        at = slice(n * PIECE, (n + 1) * PIECE)
        head = jnp.dot(GS[...], H[:, :, :, :, at].reshape(TOK, PIECE), preferred_element_type=F32)
        looked = jnp.dot(LK[...], C[:, :, :, :, at].reshape(TOK, PIECE), preferred_element_type=F32)
        ge[:, at] = (head + normalizer * looked).astype(BF16)

    p1(0)
    r1(0)
    p1(1)
    gat_c.s4(1)
    r1(1)
    p1(2)
    gat_c.s4(2)
    gat_c.s4z(0)
    vv[2].wait_recv()
    value_step(3, dev(dy=2))
    r2(0)
    r1(2)
    gat_c.s4z(1)
    gat_c.s5(0)
    embed(0)
    embed(3)
    r2(1)
    r3(0)
    gat_c.s4z(2)
    gat_c.s5(1)
    embed(1)
    r2(2)
    r3(1)
    r4(0)
    embed(4)
    gat_c.s5(2)
    flush()
    r3(2)
    r4(1)
    embed(2)
    r4(2)
    embed(5)

    vv[3].wait_recv()
    for k in range(D // 128):
        at = slice(k * 128, (k + 1) * 128)
        gv[k : k + 1, :] = VB[3, :, at] + VR[3, :, at]

    for k in range(3):
        r6(k)

    assert counter[0] <= SENDS, counter[0]
    flush()
    for k in range(3):
        for i in range(1, 4):
            z_copy(k, i).wait_send()

    @pl.when(away == 1)
    def _():
        for k in range(3):
            z_copy(k, 0).wait_send()

    @pl.when(away == 0)
    def _():
        for k in range(3):
            for dx, i in others:
                o_copy(k, dx, i).wait_send()

        @pl.when(tok_core != c)
        def _():
            for k in range(3):
                o_copy(k, 0, 0).wait_send()


def local(hidden_states, embedding, token_ids, target_ids, coefficients, cotangent, value_weight, returns):
    vmem, anywhere = pl.BlockSpec(memory_space=pltpu.VMEM), pl.BlockSpec(memory_space=pl.ANY)
    V, dma = pltpu.VMEM, pltpu.SemaphoreType.DMA
    ge, gh, gv = pl.pallas_call(
        kernel,
        out_shape=(
            pltpu.VMEM((VOC, D), BF16),
            pltpu.VMEM((ROWS, D), BF16),
            pltpu.VMEM((D // 128, 128), F32),
        ),
        in_specs=[anywhere, anywhere, vmem, vmem, vmem, anywhere, vmem, vmem],
        out_specs=(vmem, vmem, vmem),
        scratch_shapes=[
            V((4, 2, 2, ROWS, D), BF16),
            V((4, 2, 2, ROWS, D), BF16),
            V((VOC, D), BF16),
            V((2 * VOC, HALF), BF16),
            V((VOC, TOK), F32),
            V((VOC, TOK), BF16),
            V((4, 2, 2, ROWS, 2 * VOC), BF16),
            V((3, 2, 2, ROWS, QUART), F32),
            V((3, 4, 2, 2, ROWS, QUART), F32),
            V((3, 4, 2, 2, ROWS, QUART), BF16),
            V((3, 4, 2, 2, ROWS, QUART), BF16),
            V((3, 3, 2, 2, ROWS, QUART), BF16),
            V((3, 3, 4, ROWS, QUART), BF16),
            V((3, 2, 2, ROWS, QUART), BF16),
            V((3, 4, ROWS, QUART), BF16),
            V((3, 3, ROWS, QUART), BF16),
            V((3, 3, ROWS, QUART), BF16),
            V((3, 2, 2, 16, QUART), BF16),
            V((3, 8, 16, QUART), BF16),
            V((3, 16, QUART), BF16),
            V((3, 2, 2, 2, 16, QUART), BF16),
            V((4, 2, 2, 8, 128), F32),
            V((2, TOK), F32),
            V((16, 2, TOK), F32),
            V((2, TOK), F32),
            V((16, 2, TOK), F32),
            V((4, 1, D), F32),
            V((4, 1, D), F32),
            V((1, D), F32),
            V((VOC, TOK), BF16),
            dma((SENDS,)),
            dma((SENDS,)),
            dma((10,)),
        ],
        compiler_params=pltpu.CompilerParams(
            collective_id=0, has_side_effects=True, vmem_limit_bytes=50 << 20
        ),
        name="policy_head",
    )(
        hidden_states, embedding, token_ids.reshape(1, ROWS), target_ids.reshape(1, ROWS),
        coefficients.reshape(1, ROWS), cotangent, value_weight.reshape(D // 128, 128), returns.reshape(1, ROWS),
    )
    return ge, gh, gv.reshape(D)


def solution(mesh):
    in_specs = (
        P("tensor", None),
        P(("pipe", "tensor"), None),
        P("tensor"),
        P("tensor"),
        P("tensor"),
        P("tensor", None),
        P(),
        P("tensor"),
    )
    out_specs = (P(("pipe", "tensor"), None), P("tensor", None), P())
    return jax.shard_map(local, mesh=mesh, in_specs=in_specs, out_specs=out_specs, check_vma=False)
```

```python
import math

import jax
import jax.numpy as jnp
from jax import lax
from jax.experimental import pallas as pl
from jax.experimental.pallas import tpu as pltpu
from jax.sharding import PartitionSpec as P

VALUE_SCALE = 0.5
MESH = pl.DeviceIdType.MESH
F32, BF16 = jnp.float32, jnp.bfloat16

ROWS = 32
TOK = 512
D = 4608
HALF = D // 2
PIECE = 768
QUART = PIECE // 2
VOC = 640
W = HALF // 2
SENDS = 256
WIDE = 512
PARTS = ((0, 512), (512, 384), (896, 256))


def align(value, to=128):
    return pl.multiple_of(value, to)


def kernel(
    hs, emb, tid, tgt, coef, cot, vw, ret,
    ge, gh, gv,
    H, C, E, EH, LT, GS, GT, PA, PB, SA, SB, RA, RB, SA2, SB2, RA2, RB2,
    ZS, ZR, FZ, OUT, META, STA, RSA, STB, RSB, VB, VR, VW, LK,
    ss, rs, ls,
):
    pipe, tensor = lax.axis_index("pipe"), lax.axis_index("tensor")
    x, zh = pipe // 4, pipe % 4
    zl, y, c = tensor // 8, (tensor // 2) % 4, tensor % 2
    z = 2 * zh + zl
    q = x % 2

    def dev(dx=0, dy=0, dz=0, dc=0):
        xx, yy, zz, cc = (x + dx) % 4, (y + dy) % 4, (z + dz + 8) % 8, (c + dc) % 2
        return xx * 4 + zz // 2, (zz % 2) * 8 + yy * 2 + cc

    pair = 1 - 2 * zl

    counter = [0]
    started = []

    def send(src, dst, target):
        k = counter[0]
        counter[0] += 1
        cp = pltpu.make_async_remote_copy(
            src_ref=src, dst_ref=dst, send_sem=ss.at[k], recv_sem=rs.at[k],
            device_id=target, device_id_type=MESH,
        )
        cp.start()
        started.append(cp)
        return cp

    gone = set()

    def left(cp):
        if id(cp) not in gone:
            gone.add(id(cp))
            cp.wait_send()

    def flush(first=None):
        for cp in started[:first]:
            left(cp)

    def load(src, dst, k):
        cp = pltpu.make_async_copy(src, dst, ls.at[k])
        cp.start()
        return cp

    my_half = pl.ds(align(c * HALF), HALF)
    sib_half = pl.ds(align((1 - c) * HALF), HALF)
    ld_h = load(hs, H.at[0, 0, 0], 0)
    ld_e = load(emb, E, 1)
    ld_c = load(cot, C.at[0, 0, 0], 2)
    ld_eh = load(emb.at[:, my_half], EH.at[0:VOC], 3)

    plane = [(dx, dy) for dx in range(4) for dy in range(4) if (dx, dy) != (0, 0)]
    column = [(dz, dc) for dz in range(8) for dc in range(2) if (dz, dc) != (0, 0)]
    plane.sort(key=lambda d: -min(d[0], 4 - d[0]) - min(d[1], 4 - d[1]))
    column.sort(key=lambda d: -min(d[0], 8 - d[0]))
    peers = [(d, 0, 0, 0) for d in (1, 2, 3)] + [(0, d, 0, 0) for d in (1, 2, 3)]
    peers += [(0, 0, d, 0) for d in range(1, 8)] + [(0, 0, 0, 1)]
    bar = pltpu.get_barrier_semaphore()
    for peer in peers:
        pl.semaphore_signal(bar, inc=1, device_id=dev(*peer), device_id_type=MESH)

    META[0, 0, 0] = jnp.zeros((8, 128), F32)
    META[0, 0, 0, 0:1, 0:ROWS] = tid[...].astype(F32)
    META[0, 0, 0, 1:2, 0:ROWS] = tgt[...].astype(F32)
    META[0, 0, 0, 2:3, 0:ROWS] = coef[...].astype(F32)
    pl.semaphore_wait(bar, len(peers))

    def cols(half, j):
        return pl.ds(align(half * HALF + j * PIECE), PIECE)

    def quarter(half, j, k):
        return pl.ds(align(half * HALF + j * PIECE + k * QUART), QUART)

    class Gather:
        def __init__(self, X, by_z):
            self.X, self.by_z = X, by_z
            self.m = {}

        def again(self, key, part):
            pltpu.make_async_remote_copy(
                src_ref=part, dst_ref=part, send_sem=ss.at[self.m[key]], recv_sem=rs.at[self.m[key]],
                device_id=dev(dc=1), device_id_type=MESH,
            ).wait_recv()

        def own(self):
            self.m["s0"] = send(self.X.at[0, 0, 0], self.X.at[0, 0, 1], dev(dc=1))

        def gate(self, j):
            for dz in range(1 if self.by_z[j] else 2):
                for dy in (1, 3, 2):
                    left(self.m["y", dz, dy, j])

        def zsend(self, j):
            X, m = self.X, self.m
            m["za", j] = send(X.at[0, 0, 0, :, cols(q, j)], X.at[0, 1, 0, :, cols(q, j)], dev(dz=1))
            m["zb", j] = send(X.at[0, 0, 0, :, cols(1 - q, j)], X.at[0, 1, 0, :, cols(1 - q, j)], dev(dz=-1))

        def ysend(self, dz, j):
            X, m = self.X, self.m
            for dy in (1, 3, 2):
                part = X.at[0, dz, 0, :, cols(q, j)]
                m["y", dz, dy, j] = send(part, X.at[dy, dz, 0, :, cols(q, j)], dev(dy=-dy))

        def s0(self, j):
            self.m["za", j].wait_recv()
            self.ysend(1, j)

        def s1(self, j):
            X, m = self.X, self.m
            if self.by_z[j]:
                m["za", j].wait_recv()
            m["zb", j].wait_recv()
            for h, k in ((q, "sza"), (1 - q, "szb")):
                m[k, j] = send(X.at[0, 1, 0, :, cols(h, j)], X.at[0, 1, 1, :, cols(h, j)], dev(dc=1))

        def relay(self, dz, j):
            X, m = self.X, self.m
            for dy in (1, 2, 3):
                m["y", dz, dy, j].wait_recv()
            rows = pl.ds(1, 3)
            for k, dx in ((0, 1), (1, -1)):
                part = X.at[rows, dz, 0, :, quarter(q, j, k)]
                m["x", dz, k, j] = counter[0]
                send(part, part, dev(dx=dx))
            if self.by_z[j]:
                m["zc", j] = send(X.at[rows, 0, 0, :, cols(q, j)], X.at[rows, 1, 0, :, cols(q, j)], dev(dz=1))
            m["sy", dz, j] = send(
                X.at[rows, dz, 0, :, cols(q, j)], X.at[rows, dz, 1, :, cols(q, j)], dev(dc=1)
            )

        def s4(self, j):
            X, m = self.X, self.m
            rows = pl.ds(1, 3)
            for dz in range(1 if self.by_z[j] else 2):
                for k in range(2):
                    self.again(("x", dz, k, j), X.at[rows, dz, 0, :, quarter(1 - q, j, k)])
                part = cols(1 - q, j)
                if self.by_z[j]:
                    m["zd", j] = send(X.at[rows, 0, 0, :, part], X.at[rows, 1, 0, :, part], dev(dz=-1))
                m["sx", dz, j] = send(X.at[rows, dz, 0, :, part], X.at[rows, dz, 1, :, part], dev(dc=1))

        def s4z(self, j):
            X, m = self.X, self.m
            rows = pl.ds(1, 3)
            for key, back, h in (("zc", "sy", q), ("zd", "sx", 1 - q)):
                m[key, j].wait_recv()
                part = cols(h, j)
                m[back, 1, j] = send(X.at[rows, 1, 0, :, part], X.at[rows, 1, 1, :, part], dev(dc=1))

        def s5(self, j):
            m = self.m
            if j == 0:
                m["s0"].wait_recv()
            for k in ("sza", "szb"):
                m[k, j].wait_recv()
            for dz in range(2):
                m["sy", dz, j].wait_recv()
                m["sx", dz, j].wait_recv()

    gat_h, gat_c = Gather(H, (True, False, False)), Gather(C, (True, True, True))

    ld_h.wait()
    gat_h.zsend(1)
    gat_h.ysend(0, 0)
    gat_h.zsend(2)
    gat_h.zsend(0)
    gat_h.own()
    eh_s = send(emb.at[:, sib_half], EH.at[VOC : 2 * VOC], dev(dc=1))

    h_own = H[0, 0, 0].astype(F32)
    for k in range(D // 128):
        VW[:, k * 128 : (k + 1) * 128] = vw[k : k + 1, :].astype(F32)
    value_out = jnp.sum(h_own * VW[...], axis=1, keepdims=True)
    eye = lax.broadcasted_iota(jnp.int32, (ROWS, ROWS), 0) == lax.broadcasted_iota(jnp.int32, (ROWS, ROWS), 1)
    ret_col = jnp.sum(jnp.where(eye, jnp.broadcast_to(ret[...], (ROWS, ROWS)), 0.0), axis=1, keepdims=True)
    delta = VALUE_SCALE * (value_out - ret_col)
    META[0, 0, 0, 3:4, 0:ROWS] = jnp.sum(jnp.where(eye, delta, 0.0), axis=0, keepdims=True)
    VB[0] = jnp.sum(delta * h_own, axis=0, keepdims=True)
    me_s = send(META.at[0, 0, 0], META.at[0, 0, 1], dev(dc=1))
    vv = [send(VB.at[0], VR.at[0], dev(dc=1))]

    gat_h.gate(0)
    gat_h.ysend(0, 1)
    gat_h.s0(1)
    gat_h.relay(0, 0)
    gat_h.s1(1)
    gat_h.gate(1)
    gat_h.ysend(0, 2)
    gat_h.s0(2)
    gat_h.relay(0, 1)
    gat_h.relay(1, 1)
    gat_h.s4(0)
    gat_h.s1(0)
    gat_h.s1(2)
    me_s.wait_recv()
    me_z = send(META.at[0, 0], META.at[0, 1], dev(dz=pair))
    gat_h.relay(0, 2)
    gat_h.s4(1)
    gat_h.relay(1, 2)
    ld_c.wait()
    gat_c.ysend(0, 0)
    gat_h.s4z(0)
    me_z.wait_recv()
    me_y = [send(META.at[0], META.at[dy], dev(dy=-dy)) for dy in (1, 2, 3)]
    vv[0].wait_recv()

    def value_step(k, target):
        VB[k] = VB[k - 1] + VR[k - 1]
        vv.append(send(VB.at[k], VR.at[k], target))

    value_step(1, dev(dz=pair))
    gat_h.s5(0)

    def logits(j):
        def tile(n, _):
            total = jnp.zeros((VOC, 256), F32)
            for half in range(2):
                at = half * HALF + j * PIECE
                rows = H[pl.ds(2 * n, 2), :, :, :, at : at + PIECE].reshape(256, PIECE)
                total += lax.dot_general(
                    E[:, at : at + PIECE], rows, (((1,), (1,)), ((), ())), preferred_element_type=F32
                )
            where = (slice(None), pl.ds(align(n * 256, 256), 256))
            LT[where] = total if j == 0 else LT[where] + total
            return 0

        lax.fori_loop(0, 2, tile, 0)

    ld_e.wait()
    logits(0)
    gat_h.s5(1)
    logits(1)
    gat_h.s4(2)
    vv[1].wait_recv()
    value_step(2, dev(dy=1 - 2 * (y % 2)))
    gat_c.gate(0)
    gat_c.ysend(0, 1)
    gat_c.zsend(0)
    gat_h.s5(2)
    logits(2)

    peak = jnp.max(LT[...], axis=0, keepdims=True)
    weights = jnp.exp(LT[...] - peak)
    LT[...] = weights
    total = jnp.sum(weights, axis=0, keepdims=True)
    own_peak = peak
    STA[0:1] = peak
    STA[1:2] = total
    before_stats = len(started)
    sta = {}
    for dx, dy in plane:
        back = (-dx % 4) * 4 + (-dy % 4)
        sta[back] = send(STA, RSA.at[back], dev(dx=dx, dy=dy))

    def merge(stats):
        peaks = stats[0][0]
        for p, _ in stats[1:]:
            peaks = jnp.maximum(peaks, p)
        sums = sum(s * jnp.exp(p - peaks) for p, s in stats)
        return peaks, sums

    flush(before_stats)
    gat_c.ysend(0, 2)
    gat_c.relay(0, 0)
    gat_c.own()

    stats = [(peak, total)]
    for dx, dy in reversed(plane):
        k = dx * 4 + dy
        sta[k].wait_recv()
        got = RSA[k]
        if dy:
            got = jnp.concatenate([got[:, 128 * (4 - dy) :], got[:, : 128 * (4 - dy)]], axis=1)
        stats.append((got[0:1], got[1:2]))
    peak, total = merge(stats)
    STB[0:1] = peak
    STB[1:2] = total
    stb = {}
    for dz, dc in column:
        back = (-dz % 8) * 2 + dc
        stb[back] = send(STB, RSB.at[back], dev(dz=dz, dc=dc))

    gat_c.s1(0)
    gat_c.relay(0, 1)
    gat_c.zsend(1)
    gat_c.zsend(2)
    gat_c.s4(0)

    lane = lax.broadcasted_iota(jnp.int32, (2, 128), 1)

    def reorder(p, s, odd, dc):
        both = jnp.concatenate([p, s], axis=0)
        groups = []
        for g in range(4):
            part = both[:, 128 * g : 128 * (g + 1)]
            if odd:
                part = pltpu.roll(part, 64, 1)
            if dc:
                part = jnp.where((lane // 32) % 2 == 0, pltpu.roll(part, 96, 1), pltpu.roll(part, 32, 1))
            groups.append(part)
        both = jnp.concatenate(groups, axis=1)
        return both[0:1], both[1:2]

    classes = []
    for odd in range(2):
        for dc in range(2):
            stats = []
            for dz in range(odd, 8, 2):
                k = dz * 2 + dc
                if k == 0:
                    stats.append((peak, total))
                    continue
                stb[k].wait_recv()
                got = RSB[k]
                stats.append((got[0:1], got[1:2]))
            classes.append(reorder(*merge(stats), odd, dc))
    peak, total = merge(classes)

    for cp in me_y:
        cp.wait_recv()

    def facts():
        groups = []
        for dy in range(4):
            part = META[dy, 0, 0]
            for k in range(1, 4):
                part = part + pltpu.roll(META[dy, k // 2, k % 2], 32 * k, 1)
            groups.append(part)
        return jnp.concatenate(groups, axis=1)

    fact = facts()
    offset = (pipe * 16 + tensor) * VOC
    coefs, target, token = fact[2:3], fact[1:2], fact[0:1]
    factor = jnp.exp(own_peak - peak) / total
    gts = []
    for i in range(5):
        rows = pl.ds(i * 128, 128)
        vocab = (offset + i * 128 + lax.broadcasted_iota(jnp.int32, (128, 1), 0)).astype(F32)
        hit = (target == vocab).astype(F32)
        grad = (coefs * (LT[rows, :] * factor - hit)).astype(BF16)
        GS[rows, :] = grad
        turned = grad.T
        GT[:, :, :, :, i * 128 : (i + 1) * 128] = turned.reshape(4, 2, 2, ROWS, 128)
        if i in (2, 4):
            done = (0, 384) if i == 2 else (384, 256)
            for k in range(2):
                here, there = pl.ds(*done), pl.ds(VOC + done[0], done[1])
                gts.append(send(GT.at[:, :, k, :, here], GT.at[:, :, 1 - k, :, there], dev(dc=1)))
    gat_c.s1(1)
    gat_c.s1(2)
    gat_c.relay(0, 2)
    eh_s.wait_recv()
    ld_eh.wait()
    for cp in gts:
        cp.wait_recv()

    def block_of(dx):
        xx = (x + dx) % 4
        return (xx // 2 + zl) % 2, (xx % 2 + c) % 2

    dz0, dc0 = block_of(0)
    away = (x // 2 + zl) % 2
    tok_core = x % 2
    ra, rb, ra2, rb2, zk, gk = {}, {}, {}, {}, {}, {}
    others = [(dx, i) for dx in (2, 1, 3, 0) for i in (2, 1, 3, 0) if (dx, i) != (0, 0)]

    def partial(k, base):
        first, wide = PARTS[k]
        at = slice(base + first, base + first + wide)
        return jnp.dot(
            GT[...].reshape(TOK, 2 * VOC), EH[:, at], preferred_element_type=F32
        ).reshape(4, 2, 2, ROWS, wide)

    def p1a(k):
        got = partial(k, 0)
        PA[k, :, :, :, : got.shape[-1]] = got[0]
        SA[k, ..., : got.shape[-1]] = got.astype(BF16)

    def p1b(k):
        got = partial(k, W)
        PB[k, ..., : got.shape[-1]] = got
        SB[k, ..., : got.shape[-1]] = got.astype(BF16)

    def r1a(k):
        wide = pl.ds(0, PARTS[k][1])
        ra[k] = [
            send(SA.at[k, dy, :, :, :, wide], RA.at[k, dy - 1, :, :, :, wide], dev(dy=dy)) for dy in (1, 3, 2)
        ]

    def r1b(k):
        wide = pl.ds(0, PARTS[k][1])
        rb[k] = []
        for dx in (1, 3, 2):
            dz, dc = block_of(dx)
            rb[k].append(send(SB.at[k, :, dz, dc, :, wide], RB.at[k, dx - 1, :, :, wide], dev(dx=dx)))

    def r2(k):
        wide = pl.ds(0, PARTS[k][1])
        for cp in ra[k]:
            cp.wait_recv()
        total = PA[k, :, :, :, wide]
        for i in range(3):
            total += RA[k, i, :, :, :, wide].astype(F32)
        PA[k, :, :, :, wide] = total
        SA2[k, :, :, :, wide] = total.astype(BF16)
        ra2[k] = []
        for dx in (1, 3, 2):
            dz, dc = block_of(dx)
            ra2[k].append(send(SA2.at[k, dz, dc, :, wide], RA2.at[k, dx - 1, :, wide], dev(dx=dx)))
        for cp in rb[k]:
            cp.wait_recv()
        total = PB[k, :, dz0, dc0, :, wide]
        for i in range(3):
            total += RB[k, i, :, :, wide].astype(F32)
        PB[k, 0, 0, 0, :, wide] = total[0]
        SB2[k, :, :, wide] = total.astype(BF16)
        rb2[k] = [send(SB2.at[k, dy, :, wide], RB2.at[k, dy - 1, :, wide], dev(dy=dy)) for dy in (1, 3, 2)]

    def z_copy(k, i):
        zz = (z + away + 2 * i) % 8
        piece = zz // 2
        slot = away * 4 + i
        wide = pl.ds(0, PARTS[k][1])
        return pltpu.make_async_remote_copy(
            src_ref=ZS.at[k, piece // 2, piece % 2, :, wide], dst_ref=ZR.at[k, slot, :, wide], send_sem=ss.at[zk[k] + i],
            recv_sem=rs.at[zk[k] + slot], device_id=dev(dz=away + 2 * i), device_id_type=MESH,
        )

    def r3(k):
        n = PARTS[k][1]
        wide = pl.ds(0, n)
        for cp in ra2[k]:
            cp.wait_recv()
        total = PA[k, dz0, dc0, :, wide]
        for i in range(3):
            total += RA2[k, i, :, wide].astype(F32)
        ZS[k, 0, :, :, wide] = total.astype(BF16).reshape(2, 16, n)
        for cp in rb2[k]:
            cp.wait_recv()
        total = PB[k, 0, 0, 0, :, wide]
        for i in range(3):
            total += RB2[k, i, :, wide].astype(F32)
        ZS[k, 1, :, :, wide] = total.astype(BF16).reshape(2, 16, n)
        zk[k], gk[k] = counter[0], counter[0] + 8
        counter[0] += 24
        for i in range(1, 4):
            z_copy(k, i).start()

        @pl.when(away == 1)
        def _():
            z_copy(k, 0).start()

    def o_copy(k, dx, i):
        wide = pl.ds(0, PARTS[k][1])
        return pltpu.make_async_remote_copy(
            src_ref=FZ.at[k, :, wide], dst_ref=OUT.at[k, c, zh // 2, zh % 2, :, wide], send_sem=ss.at[gk[k] + dx * 4 + i],
            recv_sem=rs.at[gk[k] + c * 4 + zh], device_id=dev(dx, 0, 2 * i, tok_core + c), device_id_type=MESH,
        )

    def r4(k):
        first, n = PARTS[k]
        wide = pl.ds(0, n)

        @pl.when(away == 0)
        def _():
            for slot in range(1, 8):
                pltpu.make_async_remote_copy(
                    src_ref=ZR.at[k, slot, :, wide], dst_ref=ZR.at[k, slot, :, wide], send_sem=ss.at[zk[k]],
                    recv_sem=rs.at[zk[k] + slot], device_id=dev(dz=1), device_id_type=MESH,
                ).wait_recv()
            ab, rh = zh // 2, zh % 2
            acc = ZS[k, ab, rh, :, wide].astype(F32)
            for slot in range(1, 8):
                acc += ZR[k, slot, :, wide].astype(F32)
            row = META[0, 0, dc0, 3:4, :]
            lanes = lax.broadcasted_iota(jnp.int32, (16, 128), 1)
            picks = lanes == lax.broadcasted_iota(jnp.int32, (16, 128), 0) + 16 * rh
            delta16 = jnp.sum(jnp.where(picks, row, 0.0), axis=1, keepdims=True)
            weight = VW[:, pl.ds(align(c * HALF + ab * W + first), n)]
            FZ[k, :, wide] = (acc + delta16 * weight).astype(BF16)
            for dx, i in others:
                o_copy(k, dx, i).start()

            @pl.when(tok_core == c)
            def _():
                OUT[k, c, ab, rh, :, wide] = FZ[k, :, wide]

            @pl.when(tok_core != c)
            def _():
                o_copy(k, 0, 0).start()

    home = (zl * 2 + c) == x

    def r6(k):
        first, n = PARTS[k]
        wide = pl.ds(0, n)

        def o_wait(core, piece):
            pltpu.make_async_remote_copy(
                src_ref=FZ.at[k, :, wide], dst_ref=OUT.at[k, core, piece // 2, piece % 2, :, wide], send_sem=ss.at[gk[k]],
                recv_sem=rs.at[gk[k] + core * 4 + piece], device_id=dev(dx=1), device_id_type=MESH,
            ).wait_recv()

        for i in range(4):
            o_wait(1 - c, i)
        for i in range(1, 4):
            o_wait(c, (zh + i) % 4)

        @pl.when(jnp.logical_not(home))
        def _():
            o_wait(c, zh)

        for cs in range(2):
            for ab in range(2):
                at = cs * HALF + ab * W + first
                for rh in range(2):
                    gh[rh * 16 : (rh + 1) * 16, at : at + n] = OUT[k, cs, ab, rh, :, wide]

    vocab = (offset + lax.broadcasted_iota(jnp.int32, (VOC, 1), 0)).astype(F32)
    LK[...] = (token == vocab).astype(BF16)
    normalizer = math.sqrt(D)

    def embed(n):
        at = slice(n * PIECE, (n + 1) * PIECE)
        head = jnp.dot(GS[...], H[:, :, :, :, at].reshape(TOK, PIECE), preferred_element_type=F32)
        looked = jnp.dot(LK[...], C[:, :, :, :, at].reshape(TOK, PIECE), preferred_element_type=F32)
        ge[:, at] = (head + normalizer * looked).astype(BF16)

    p1a(0)
    r1a(0)
    p1b(0)
    r1b(0)
    p1a(1)
    p1b(1)
    gat_c.s4(1)
    r1a(1)
    r1b(1)
    p1a(2)
    p1b(2)
    gat_c.s4(2)
    gat_c.s4z(0)
    vv[2].wait_recv()
    value_step(3, dev(dy=2))
    r2(0)
    r1a(2)
    r1b(2)
    gat_c.s4z(1)
    gat_c.s5(0)
    embed(0)
    embed(3)
    r2(1)
    r3(0)
    gat_c.s4z(2)
    gat_c.s5(1)
    embed(1)
    r2(2)
    r3(1)
    r4(0)
    embed(4)
    gat_c.s5(2)
    flush()
    r3(2)
    r4(1)
    embed(2)
    r4(2)
    embed(5)

    vv[3].wait_recv()
    for k in range(D // 128):
        at = slice(k * 128, (k + 1) * 128)
        gv[k : k + 1, :] = VB[3, :, at] + VR[3, :, at]

    for k in range(3):
        r6(k)

    assert counter[0] <= SENDS, counter[0]
    flush()
    for k in range(3):
        for i in range(1, 4):
            z_copy(k, i).wait_send()

    @pl.when(away == 1)
    def _():
        for k in range(3):
            z_copy(k, 0).wait_send()

    @pl.when(away == 0)
    def _():
        for k in range(3):
            for dx, i in others:
                o_copy(k, dx, i).wait_send()

        @pl.when(tok_core != c)
        def _():
            for k in range(3):
                o_copy(k, 0, 0).wait_send()


def local(hidden_states, embedding, token_ids, target_ids, coefficients, cotangent, value_weight, returns):
    vmem, anywhere = pl.BlockSpec(memory_space=pltpu.VMEM), pl.BlockSpec(memory_space=pl.ANY)
    V, dma = pltpu.VMEM, pltpu.SemaphoreType.DMA
    ge, gh, gv = pl.pallas_call(
        kernel,
        out_shape=(
            pltpu.VMEM((VOC, D), BF16),
            pltpu.VMEM((ROWS, D), BF16),
            pltpu.VMEM((D // 128, 128), F32),
        ),
        in_specs=[anywhere, anywhere, vmem, vmem, vmem, anywhere, vmem, vmem],
        out_specs=(vmem, vmem, vmem),
        scratch_shapes=[
            V((4, 2, 2, ROWS, D), BF16),
            V((4, 2, 2, ROWS, D), BF16),
            V((VOC, D), BF16),
            V((2 * VOC, HALF), BF16),
            V((VOC, TOK), F32),
            V((VOC, TOK), BF16),
            V((4, 2, 2, ROWS, 2 * VOC), BF16),
            V((3, 2, 2, ROWS, WIDE), F32),
            V((3, 4, 2, 2, ROWS, WIDE), F32),
            V((3, 4, 2, 2, ROWS, WIDE), BF16),
            V((3, 4, 2, 2, ROWS, WIDE), BF16),
            V((3, 3, 2, 2, ROWS, WIDE), BF16),
            V((3, 3, 4, ROWS, WIDE), BF16),
            V((3, 2, 2, ROWS, WIDE), BF16),
            V((3, 4, ROWS, WIDE), BF16),
            V((3, 3, ROWS, WIDE), BF16),
            V((3, 3, ROWS, WIDE), BF16),
            V((3, 2, 2, 16, WIDE), BF16),
            V((3, 8, 16, WIDE), BF16),
            V((3, 16, WIDE), BF16),
            V((3, 2, 2, 2, 16, WIDE), BF16),
            V((4, 2, 2, 8, 128), F32),
            V((2, TOK), F32),
            V((16, 2, TOK), F32),
            V((2, TOK), F32),
            V((16, 2, TOK), F32),
            V((4, 1, D), F32),
            V((4, 1, D), F32),
            V((1, D), F32),
            V((VOC, TOK), BF16),
            dma((SENDS,)),
            dma((SENDS,)),
            dma((10,)),
        ],
        compiler_params=pltpu.CompilerParams(
            collective_id=0, has_side_effects=True, vmem_limit_bytes=50 << 20
        ),
        name="policy_head",
    )(
        hidden_states, embedding, token_ids.reshape(1, ROWS), target_ids.reshape(1, ROWS),
        coefficients.reshape(1, ROWS), cotangent, value_weight.reshape(D // 128, 128), returns.reshape(1, ROWS),
    )
    return ge, gh, gv.reshape(D)


def solution(mesh):
    in_specs = (
        P("tensor", None),
        P(("pipe", "tensor"), None),
        P("tensor"),
        P("tensor"),
        P("tensor"),
        P("tensor", None),
        P(),
        P("tensor"),
    )
    out_specs = (P(("pipe", "tensor"), None), P("tensor", None), P())
    return jax.shard_map(local, mesh=mesh, in_specs=in_specs, out_specs=out_specs, check_vma=False)
```
